128 devices in a mesh: lat: 8 (over x, z_hi), lon: 16 (over y, z_lo, core).
Axes of the slice: x: 4, y: 4, z: 4 (z_hi: 2, z_lo: 2; z = z_hi * 2 + z_lo), core: 2. Of those that a mesh axis runs over, the one named last changes fastest.
Arguments:
- latents: bfloat16 [2, 96, 1152, 512], P(None, 'lat', 'lon'), may hold values from -6 to 6
- attend_gain: float32 [512], replicated, may hold values from 0.1 to 1.9
- packed_heads: bfloat16 [512, 1536], P('lon'), may hold values from -4 to 4
- heads_back: bfloat16 [512, 512], P('lon'), may hold values from -0.25 to 0.25
- dense_gain: float32 [512], replicated, may hold values from 0.1 to 1.9
- expand_weight: bfloat16 [512, 2048], P('lon'), may hold values from -0.25 to 0.25
- shrink_weight: bfloat16 [2048, 512], P('lon'), may hold values from -0.125 to 0.125
- merge_gain: float32 [2048], replicated, may hold values from 0.1 to 1.9
- merge_weight: bfloat16 [2048, 1024], P('lon'), may hold values from -0.125 to 0.125
- coarse_gain: float32 [1024], replicated, may hold values from 0.1 to 1.9
- coarse_heads: bfloat16 [1024, 3072], P('lon'), may hold values from -4 to 4
- coarse_back: bfloat16 [1024, 1024], P('lon'), may hold values from -0.1875 to 0.1875
- coarse_scale: float32 [1024], replicated, may hold values from 0.1 to 1.9
- coarse_expand: bfloat16 [1024, 4096], P('lon'), may hold values from -0.1875 to 0.1875
- coarse_shrink: bfloat16 [4096, 1024], P('lon'), may hold values from -0.09375 to 0.09375
Outputs:
- coarse_latents: bfloat16 [2, 48, 576, 1024], P(None, 'lat', 'lon')
The draws below stay inside these ranges and needn't reach their ends.
All inputs are finite; a program needn't handle non-finite values.
Results may differ from the reference program's by a relative error of at most 0.034.
Values may be sent and summed in bfloat16 or wider, within the bound.
No kernel may reach another device: no remote copies, remote signals or barrier semaphores. Data moves between devices by JAX's collectives and lax.ppermute only.
A program may use at most 192 MiB of HBM per device.

```python
import math
import jax
import jax.numpy as jnp
from jax import lax

D = 512
HEAD = 64
WIN_LEV = 2
WIN_LAT = 6
WIN_LON = 12
LEV = 2
NLAT = 96
NLON = 1152


def head_columns(key, width, boost):
    base = jnp.clip(jax.random.normal(key, (width, 3 * width), jnp.float32), -6.0, 6.0) / math.sqrt(width)
    column = jnp.arange(3 * width)
    return base * jnp.where(column < 2 * width, boost, 1.0)


def draw_packed_heads(key, part):
    key = jax.random.fold_in(key, 5)
    return head_columns(key, D, 1.0).astype(jnp.bfloat16)


def draw_coarse_heads(key, part):
    key = jax.random.fold_in(key, 9)
    return head_columns(key, 2 * D, 1.0).astype(jnp.bfloat16)


def steps_of(own_key, shape, cuts, low, largest):
    level = 1.0
    for position, blocks in cuts:
        steps = jax.random.uniform(jax.random.fold_in(jax.random.fold_in(own_key, 6), position), (blocks,), jnp.float32, low / len(cuts), largest / len(cuts))
        level = level * jnp.repeat(jnp.exp(steps), shape[position] // blocks).reshape((-1,) + (1,) * (len(shape) - 1 - position))
    return level


def bell_draw(own_key, shape, scale, reach, shards=(), kind=jnp.bfloat16):
    array = jax.random.normal(own_key, shape, jnp.float32) * scale
    if len(shards) > 0:
        array = steps_of(own_key, shape, shards, -0.22, 0.18) * array
    return jnp.clip(array, min=-reach, max=reach).astype(kind)


def setup_inputs(seed: int = 0) -> dict:
    streams_of = jax.random.split(jax.random.key(seed), 16)
    return {
        "latents": bell_draw(streams_of[0], (LEV, NLAT, NLON, D), 1.0, 6.0, ((1, 8), (2, 16))),
        "attend_gain": jnp.clip(1.0 + 0.18 * jax.random.normal(streams_of[1], (D,), jnp.float32), 0.1, 1.9),
        "packed_heads": draw_packed_heads(jax.random.fold_in(streams_of[15], 71), 0),
        "heads_back": bell_draw(streams_of[3], (D, D), D ** -0.5, 0.25, ((0, 16),)),
        "dense_gain": jnp.clip(1.0 + 0.18 * jax.random.normal(streams_of[4], (D,), jnp.float32), 0.1, 1.9),
        "expand_weight": bell_draw(streams_of[5], (D, 4 * D), D ** -0.5, 0.25, ((0, 16),)),
        "shrink_weight": bell_draw(streams_of[6], (4 * D, D), (4 * D) ** -0.5, 0.125, ((0, 16),)),
        "merge_gain": jnp.clip(1.0 + 0.18 * jax.random.normal(streams_of[7], (4 * D,), jnp.float32), 0.1, 1.9),
        "merge_weight": bell_draw(streams_of[8], (4 * D, 2 * D), (4 * D) ** -0.5, 0.125, ((0, 16),)),
        "coarse_gain": jnp.clip(1.0 + 0.18 * jax.random.normal(streams_of[9], (2 * D,), jnp.float32), 0.1, 1.9),
        "coarse_heads": draw_coarse_heads(jax.random.fold_in(streams_of[15], 71), 0),
        "coarse_back": bell_draw(streams_of[11], (2 * D, 2 * D), (2 * D) ** -0.5, 0.1875, ((0, 16),)),
        "coarse_scale": jnp.clip(1.0 + 0.18 * jax.random.normal(streams_of[12], (2 * D,), jnp.float32), 0.1, 1.9),
        "coarse_expand": bell_draw(streams_of[13], (2 * D, 8 * D), (2 * D) ** -0.5, 0.1875, ((0, 16),)),
        "coarse_shrink": bell_draw(streams_of[14], (8 * D, 2 * D), (8 * D) ** -0.5, 0.09375, ((0, 16),)),
    }


EPS = 1e-05
SCALE = 0.125

def layer_norm(values, gain):
    values = values.astype(jnp.float32)
    center = values - lax.optimization_barrier(jnp.mean(values, -1, keepdims=True))
    spread = lax.optimization_barrier(jnp.mean(center * center, -1, keepdims=True))
    return center * lax.rsqrt(spread + EPS) * gain.astype(jnp.float32)

def window_split(grid):
    levels, rows, cols, width = grid.shape
    parts = grid.reshape(levels // WIN_LEV, WIN_LEV, rows // WIN_LAT, WIN_LAT, cols // WIN_LON, WIN_LON, width)
    parts = parts.transpose(0, 2, 4, 1, 3, 5, 6)
    return parts.reshape(-1, WIN_LEV * WIN_LAT * WIN_LON, width)

def window_join(parts, levels, rows, cols):
    width = parts.shape[-1]
    grid = parts.reshape(levels // WIN_LEV, rows // WIN_LAT, cols // WIN_LON, WIN_LEV, WIN_LAT, WIN_LON, width)
    return grid.transpose(0, 3, 1, 4, 2, 5, 6).reshape(levels, rows, cols, width)

def matmul(rows, weight):
    return jnp.dot(rows, weight, preferred_element_type=jnp.float32)

def attention(parts, flags, gain, packed, back):
    groups, count, width = parts.shape
    heads = width // HEAD
    flat = parts.reshape(-1, width)
    normed = layer_norm(flat, gain).astype(jnp.bfloat16)
    qkv = matmul(normed, packed).astype(jnp.bfloat16)
    qkv = qkv.reshape(groups, count, 3, heads, HEAD).astype(jnp.float32)
    scores = jnp.einsum('gqhe,gkhe->ghqk', qkv[:, :, 0], qkv[:, :, 1]) * SCALE
    same = flags[:, :, None] == flags[:, None, :]
    scores = jnp.where(same[:, None], scores, -1e+30)
    top = lax.optimization_barrier(jnp.max(scores, -1, keepdims=True))
    weights = jnp.exp(scores - top)
    probs = (weights / lax.optimization_barrier(jnp.sum(weights, -1, keepdims=True))).astype(jnp.bfloat16)
    context = jnp.einsum('ghqk,gkhe->gqhe', probs.astype(jnp.float32), qkv[:, :, 2]).astype(jnp.bfloat16)
    return (flat.astype(jnp.float32) + matmul(context.reshape(-1, width), back)).astype(jnp.bfloat16)

def dense(flat, gain, expand, shrink):
    hidden = layer_norm(flat, gain).astype(jnp.bfloat16)
    expanded = jax.nn.gelu(matmul(hidden, expand), approximate=False).astype(jnp.bfloat16)
    return (flat.astype(jnp.float32) + matmul(expanded, shrink)).astype(jnp.bfloat16)

def section(grid, flag_rows, weights):
    levels, rows, cols, width = grid.shape
    bands = grid.reshape(levels, rows // WIN_LAT, WIN_LAT, cols, width).transpose(1, 0, 2, 3, 4)

    def one_band(item):
        band, band_flags = item
        parts = window_split(band)
        spread_flags = jnp.broadcast_to(band_flags[None, :, None, None], (levels, WIN_LAT, cols, 1))
        token_flags = window_split(spread_flags)[:, :, 0]
        mixed = attention(parts, token_flags, weights[0], weights[1], weights[2])
        done = dense(mixed, weights[3], weights[4], weights[5])
        return window_join(done.reshape(parts.shape), levels, WIN_LAT, cols)
    finished = lax.map(one_band, (bands, flag_rows))
    return finished.transpose(1, 0, 2, 3, 4).reshape(levels, rows, cols, width)

def merge(grid, gain, weight):
    levels, rows, cols, width = grid.shape
    quads = grid.reshape(levels, rows // 2, 2, cols // 2, 2, width).transpose(0, 1, 3, 4, 2, 5)
    quads = quads.reshape(-1, 4 * width)
    normed = layer_norm(quads, gain).astype(jnp.bfloat16)
    return matmul(normed, weight).astype(jnp.bfloat16).reshape(levels, rows // 2, cols // 2, -1)

def reference(latents, attend_gain, packed_heads, heads_back, dense_gain, expand_weight, shrink_weight, merge_gain, merge_weight, coarse_gain, coarse_heads, coarse_back, coarse_scale, coarse_expand, coarse_shrink):
    total_rows = latents.shape[1]
    lat_cut = WIN_LAT // 2
    lon_cut = WIN_LON // 2
    rolled = jnp.roll(latents, (-lat_cut, -lon_cut), axis=(1, 2))
    row_ids = jnp.arange(total_rows, dtype=jnp.int32)
    flag_rows = (row_ids >= total_rows - lat_cut).astype(jnp.int32).reshape(-1, WIN_LAT)
    first = section(rolled, flag_rows, (attend_gain, packed_heads, heads_back, dense_gain, expand_weight, shrink_weight))
    first = jnp.roll(first, (lat_cut, lon_cut), axis=(1, 2))
    merged = merge(first, merge_gain, merge_weight)
    zero_rows = jnp.zeros((merged.shape[1] // WIN_LAT, WIN_LAT), jnp.int32)
    return section(merged, zero_rows, (coarse_gain, coarse_heads, coarse_back, coarse_scale, coarse_expand, coarse_shrink))
```

```python
import functools
import jax
import jax.numpy as jnp
from jax import lax
from jax.experimental import pallas as pl
from jax.experimental.pallas import tpu as pltpu
from jax.sharding import Mesh, PartitionSpec as P

HEAD = 64
COUNT = 144
WIN_LEV = 2
WIN_LAT = 6
WIN_LON = 12
EPS = 1e-05
SCALE = 0.125
VMEM_LIMIT = 56 * 1024 * 1024
F32 = jnp.float32
BF16 = jnp.bfloat16


def normalize(values, gain):
    center = values - jnp.mean(values, -1, keepdims=True)
    spread = jnp.mean(center * center, -1, keepdims=True)
    return center * lax.rsqrt(spread + EPS) * gain


def dot(left, right):
    return jnp.dot(left, right, preferred_element_type=F32)


def gelu(x):
    return 0.5 * x * (1.0 + lax.erf(x * (0.5 ** 0.5)))


def fetch(order, buffers, place, semaphore):
    copies = []
    position = 0
    for buffer in buffers:
        for item in range(buffer.shape[0]):
            for source, target in place(buffer.at[item], order[position]):
                copies.append(pltpu.make_async_copy(source, target, semaphore))
            position += 1
    for copy in copies:
        copy.start()
    return copies


def await_all(copies):
    for copy in copies:
        copy.wait()


def attend_kernel(heads, windows, masked, order, x_ref, bias_ref, gain_ref, *rest):
    *buffers, out_ref, weights, qkv, context, semaphore = rest
    width = heads * HEAD
    share = width // 16
    first = pl.program_id(0) == 0

    @pl.when(first)
    def _():
        def place(block, index):
            rows = pl.ds(pl.multiple_of(index * share, share), share)
            return [(block, weights.at[:, rows, :])]

        await_all(fetch(order, buffers, place, semaphore))

    normed = normalize(x_ref[...].astype(F32), gain_ref[...]).astype(BF16)
    qkv[:, :width] = (dot(normed, weights[0]) * SCALE).astype(BF16)
    qkv[:, width : 2 * width] = dot(normed, weights[1]).astype(BF16)
    qkv[:, 2 * width :] = dot(normed, weights[2]).astype(BF16)

    low = lax.broadcasted_iota(jnp.int32, (COUNT, 128), 1) < HEAD
    zero = jnp.zeros((COUNT, 128), BF16)
    one = jnp.ones((COUNT, 128), BF16)

    def window(index, _):
        rows = pl.ds(pl.multiple_of(index * COUNT, COUNT), COUNT)
        for pair in range(heads // 2):
            lanes = slice(pair * 128, pair * 128 + 128)
            q = qkv[rows, lanes]
            k = qkv[rows, width + pair * 128 : width + pair * 128 + 128]
            v = qkv[rows, 2 * width + pair * 128 : 2 * width + pair * 128 + 128]
            results = []
            for half in range(2):
                mine = low if half == 0 else jnp.logical_not(low)
                scores = lax.dot_general(
                    q, jnp.where(mine, k, zero), (((1,), (1,)), ((), ())), preferred_element_type=F32
                )
                if masked:
                    scores = scores + bias_ref[...]
                powers = jnp.exp(scores - jnp.max(scores, -1, keepdims=True)).astype(BF16)
                results.append(dot(powers, jnp.where(mine, v, one)))
            upper = jnp.where(low, results[0], results[1])
            lower = jnp.where(low, results[1], results[0])
            context[rows, lanes] = (upper / pltpu.roll(lower, HEAD, 1)).astype(BF16)
        return 0

    lax.fori_loop(0, windows, window, 0)
    out_ref[...] = (x_ref[...].astype(F32) + dot(context[...], weights[3])).astype(BF16)


def any_specs(buffers):
    return [pl.BlockSpec(memory_space=pl.ANY)] * len(buffers)


def params():
    return pltpu.CompilerParams(
        dimension_semantics=("arbitrary",), vmem_limit_bytes=VMEM_LIMIT
    )


def attend(x, bias, gain, order, buffers, heads, steps):
    tokens, width = x.shape
    tile = tokens // steps
    masked = bias is not None
    if not masked:
        bias = jnp.zeros((1, COUNT, COUNT), F32)
    picks = bias.shape[0] > 1
    return pl.pallas_call(
        functools.partial(attend_kernel, heads, tile // COUNT, masked),
        out_shape=jax.ShapeDtypeStruct(x.shape, BF16),
        grid=(steps,),
        in_specs=[
            pl.BlockSpec(memory_space=pltpu.SMEM),
            pl.BlockSpec((tile, width), lambda i: (i, 0)),
            pl.BlockSpec((None, COUNT, COUNT), lambda i: (i if picks else 0, 0, 0)),
            pl.BlockSpec((1, width), lambda i: (0, 0)),
        ]
        + any_specs(buffers),
        out_specs=pl.BlockSpec((tile, width), lambda i: (i, 0)),
        scratch_shapes=[
            pltpu.VMEM((4, width, width), BF16),
            pltpu.VMEM((tile, 3 * width), BF16),
            pltpu.VMEM((tile, width), BF16),
            pltpu.SemaphoreType.DMA,
        ],
        compiler_params=params(),
        cost_estimate=pl.CostEstimate(
            flops=8 * tokens * width * width + 4 * tokens * COUNT * width,
            bytes_accessed=8 * width * width + 4 * tokens * width,
            transcendentals=tokens * COUNT * heads,
        ),
    )(order, x, bias, gain.reshape(1, -1), *buffers)


def dense_kernel(order, x_ref, gain_ref, *rest):
    *buffers, out_ref, expand, shrink, semaphore = rest
    width = x_ref.shape[1]
    share = width // 16

    @pl.when(pl.program_id(0) == 0)
    def _():
        def place(block, index):
            rows = pl.ds(pl.multiple_of(index * share, share), share)
            return [
                (block.at[pl.ds(0, 4)], expand.at[:, rows, :]),
                (block.at[pl.ds(4, 4)], shrink.at[pl.ds(index * 4, 4)]),
            ]

        await_all(fetch(order, buffers, place, semaphore))

    x = x_ref[...].astype(F32)
    hidden = normalize(x, gain_ref[...]).astype(BF16)
    total = x
    for part in range(4):
        grown = gelu(dot(hidden, expand[part])).astype(BF16)
        back = shrink[part * 16 : part * 16 + 16].reshape(width, width)
        total = total + dot(grown, back)
    out_ref[...] = total.astype(BF16)


def dense(x, gain, order, buffers, steps):
    tokens, width = x.shape
    tile = tokens // steps
    return pl.pallas_call(
        dense_kernel,
        out_shape=jax.ShapeDtypeStruct(x.shape, BF16),
        grid=(steps,),
        in_specs=[
            pl.BlockSpec(memory_space=pltpu.SMEM),
            pl.BlockSpec((tile, width), lambda i: (i, 0)),
            pl.BlockSpec((1, width), lambda i: (0, 0)),
        ]
        + any_specs(buffers),
        out_specs=pl.BlockSpec((tile, width), lambda i: (i, 0)),
        scratch_shapes=[
            pltpu.VMEM((4, width, width), BF16),
            pltpu.VMEM((64, width // 16, width), BF16),
            pltpu.SemaphoreType.DMA,
        ],
        compiler_params=params(),
        cost_estimate=pl.CostEstimate(
            flops=16 * tokens * width * width,
            bytes_accessed=16 * width * width + 4 * tokens * width,
            transcendentals=4 * tokens * width,
        ),
    )(order, x, gain.reshape(1, -1), *buffers)


def merge_kernel(order, x_ref, gain_ref, *rest):
    *buffers, out_ref, weights, semaphore = rest
    width = x_ref.shape[2]

    def place(block, index):
        return [(block, weights.at[pl.ds(index * 2, 2)])]

    copies = fetch(order, buffers, place, semaphore)
    quarters = [x_ref[part].astype(F32) for part in range(4)]
    mean = sum(jnp.sum(item, -1, keepdims=True) for item in quarters) / (4 * width)
    quarters = [item - mean for item in quarters]
    spread = sum(jnp.sum(item * item, -1, keepdims=True) for item in quarters) / (4 * width)
    level = lax.rsqrt(spread + EPS)
    normed = [
        (item * level * gain_ref[:, part * width : part * width + width]).astype(BF16)
        for part, item in enumerate(quarters)
    ]
    await_all(copies)
    total = dot(normed[0], weights[0:8].reshape(width, 2 * width))
    for part in range(1, 4):
        total = total + dot(normed[part], weights[part * 8 : part * 8 + 8].reshape(width, 2 * width))
    out_ref[...] = total.astype(BF16)


def merge(x, gain, order, buffers):
    _, tokens, width = x.shape
    return pl.pallas_call(
        merge_kernel,
        out_shape=jax.ShapeDtypeStruct((tokens, 2 * width), BF16),
        in_specs=[
            pl.BlockSpec(memory_space=pltpu.SMEM),
            pl.BlockSpec(memory_space=pltpu.VMEM),
            pl.BlockSpec(memory_space=pltpu.VMEM),
        ]
        + any_specs(buffers),
        out_specs=pl.BlockSpec(memory_space=pltpu.VMEM),
        scratch_shapes=[
            pltpu.VMEM((32, width // 8, 2 * width), BF16),
            pltpu.SemaphoreType.DMA,
        ],
        compiler_params=pltpu.CompilerParams(vmem_limit_bytes=VMEM_LIMIT),
        cost_estimate=pl.CostEstimate(
            flops=16 * tokens * width * width,
            bytes_accessed=16 * width * width + 12 * tokens * width,
            transcendentals=0,
        ),
    )(order, x, gain.reshape(1, -1), *buffers)


def grow_kernel(order, x_ref, gain_ref, *rest):
    *buffers, out_ref, weights, semaphore = rest
    width = x_ref.shape[1]
    share = width // 16

    def place(block, index):
        rows = pl.ds(pl.multiple_of(index * share, share), share)
        return [(block, weights.at[:, rows, :])]

    copies = fetch(order, buffers, place, semaphore)
    hidden = normalize(x_ref[...].astype(F32), gain_ref[...]).astype(BF16)
    await_all(copies)
    for part in range(4):
        for half in range(2):
            lanes = slice(half * (width // 2), (half + 1) * (width // 2))
            target = slice(part * width + half * (width // 2), part * width + (half + 1) * (width // 2))
            out_ref[:, target] = gelu(dot(hidden, weights[part, :, lanes])).astype(BF16)


def grow(x, gain, order, buffers):
    tokens, width = x.shape
    return pl.pallas_call(
        grow_kernel,
        out_shape=jax.ShapeDtypeStruct((tokens, 4 * width), BF16),
        in_specs=[
            pl.BlockSpec(memory_space=pltpu.SMEM),
            pl.BlockSpec(memory_space=pltpu.VMEM),
            pl.BlockSpec(memory_space=pltpu.VMEM),
        ]
        + any_specs(buffers),
        out_specs=pl.BlockSpec(memory_space=pltpu.VMEM),
        scratch_shapes=[pltpu.VMEM((4, width, width), BF16), pltpu.SemaphoreType.DMA],
        compiler_params=pltpu.CompilerParams(vmem_limit_bytes=VMEM_LIMIT),
        cost_estimate=pl.CostEstimate(
            flops=8 * tokens * width * width,
            bytes_accessed=8 * width * width + 10 * tokens * width,
            transcendentals=4 * tokens * width,
        ),
    )(order, x, gain.reshape(1, -1), *buffers)


def fold_kernel(order, x_ref, grown_ref, *rest):
    *buffers, out_ref, weights, semaphore = rest
    width = x_ref.shape[1]

    def place(block, index):
        return [(block, weights.at[pl.ds(index * 4, 4)])]

    await_all(fetch(order, buffers, place, semaphore))
    for half in range(2):
        lanes = slice(half * (width // 2), (half + 1) * (width // 2))
        back = weights[:, :, lanes].reshape(4 * width, width // 2)
        out_ref[:, lanes] = (x_ref[:, lanes].astype(F32) + dot(grown_ref[...], back)).astype(BF16)


def fold(x, grown, order, buffers):
    tokens, width = x.shape
    return pl.pallas_call(
        fold_kernel,
        out_shape=jax.ShapeDtypeStruct((tokens, width), BF16),
        in_specs=[
            pl.BlockSpec(memory_space=pltpu.SMEM),
            pl.BlockSpec(memory_space=pltpu.VMEM),
            pl.BlockSpec(memory_space=pltpu.VMEM),
        ]
        + any_specs(buffers),
        out_specs=pl.BlockSpec(memory_space=pltpu.VMEM),
        scratch_shapes=[pltpu.VMEM((64, width // 16, width), BF16), pltpu.SemaphoreType.DMA],
        compiler_params=pltpu.CompilerParams(vmem_limit_bytes=VMEM_LIMIT),
        cost_estimate=pl.CostEstimate(
            flops=8 * tokens * width * width,
            bytes_accessed=8 * width * width + 12 * tokens * width,
            transcendentals=0,
        ),
    )(order, x, grown, *buffers)


def gather(shard):
    whole = lax.all_gather(shard, ("y", "zl", "c"), axis=0, tiled=False)
    return whole


def in_columns(shard, parts):
    rows, columns = shard.shape
    return shard.reshape(rows, parts, columns // parts).transpose(1, 0, 2)


def in_rows(shard, parts):
    rows, columns = shard.shape
    return shard.reshape(parts, rows // parts, columns)


def passed_along(value, axes, steps):
    count = 1
    for axis in axes:
        count *= lax.axis_size(axis)
    pairs = [(source, (source + steps) % count) for source in range(count)]
    return lax.ppermute(value, axes, pairs)


LAT = ("x", "zh")
LON = ("y", "zl", "c")


def roll_lat(grid, forward):
    cut = WIN_LAT // 2
    height = grid.shape[1]
    edge = grid[:, :cut] if forward else grid[:, height - cut :]
    moved = passed_along(edge, LAT, -1 if forward else 1)
    if forward:
        return jnp.concatenate([grid[:, cut:], moved], 1)
    return jnp.concatenate([moved, grid[:, : height - cut]], 1)


def roll_lon(grid, forward):
    cut = WIN_LON // 2
    breadth = grid.shape[2]
    edge = grid[:, :, :cut] if forward else grid[:, :, breadth - cut :]
    moved = passed_along(edge, LON, -1 if forward else 1)
    if forward:
        return jnp.concatenate([grid[:, :, cut:], moved], 2)
    return jnp.concatenate([moved, grid[:, :, : breadth - cut]], 2)


def window_split(grid):
    levels, rows, cols, width = grid.shape
    parts = grid.reshape(levels, rows // WIN_LAT, WIN_LAT, cols // WIN_LON, WIN_LON, width)
    return parts.transpose(1, 3, 0, 2, 4, 5).reshape(-1, width)


def window_join(parts, rows, cols):
    width = parts.shape[-1]
    grid = parts.reshape(rows // WIN_LAT, cols // WIN_LON, WIN_LEV, WIN_LAT, WIN_LON, width)
    return grid.transpose(2, 0, 3, 1, 4, 5).reshape(WIN_LEV, rows, cols, width)


def per_device(
    latents,
    attend_gain,
    packed_heads,
    heads_back,
    dense_gain,
    expand_weight,
    shrink_weight,
    merge_gain,
    merge_weight,
    coarse_gain,
    coarse_heads,
    coarse_back,
    coarse_scale,
    coarse_expand,
    coarse_shrink,
):
    _, rows, cols, width = latents.shape
    order = jnp.arange(16, dtype=jnp.int32)
    fine_attend = [gather(jnp.concatenate([in_columns(packed_heads, 3), heads_back[None]], 0))]
    fine_dense = [gather(jnp.concatenate([in_columns(expand_weight, 4), in_rows(shrink_weight, 4)], 0))]
    merging = [gather(in_rows(merge_weight, 2))]
    coarse_attend = [gather(jnp.concatenate([in_columns(coarse_heads, 3), coarse_back[None]], 0))]
    coarse_grow = [gather(in_columns(coarse_expand, 4))]
    coarse_fold = [gather(in_rows(coarse_shrink, 4))]

    rolled = roll_lon(roll_lat(latents, True), True)
    late = (jnp.arange(COUNT) // WIN_LON) % WIN_LAT >= WIN_LAT // 2
    wall = jnp.where(late[:, None] == late[None, :], 0.0, -1e30).astype(F32)
    place = lax.axis_index("x") * 2 + lax.axis_index("zh")
    last = (place == lax.axis_size("x") * 2 - 1).astype(F32)
    bias = jnp.stack([jnp.zeros_like(wall), wall * last])

    mixed = attend(window_split(rolled), bias, attend_gain, order, fine_attend, 8, 2)
    shifted = dense(mixed, dense_gain, order, fine_dense, 4)
    first = roll_lon(roll_lat(window_join(shifted, rows, cols), False), False)
    quads = first.reshape(WIN_LEV, rows // 2, 2, cols // 24, WIN_LON, 2, width)
    quads = quads.transpose(5, 2, 3, 0, 1, 4, 6).reshape(4, -1, width)
    merged = merge(quads, merge_gain, order, merging)
    coarse_mixed = attend(merged, None, coarse_gain, order, coarse_attend, 16, 1)
    grown = grow(coarse_mixed, coarse_scale, order, coarse_grow)
    finished = fold(coarse_mixed, grown, order, coarse_fold)
    return window_join(finished, rows // 2, cols // 2)


def solution(mesh):
    fine_mesh = Mesh(mesh.devices.reshape(4, 2, 4, 2, 2), ("x", "zh", "y", "zl", "c"))
    rows = P(LON, None)
    grid = P(None, LAT, LON, None)
    in_specs = (grid, P(), rows, rows, P(), rows, rows, P(), rows, P(), rows, rows, P(), rows, rows)
    return jax.shard_map(
        per_device, mesh=fine_mesh, in_specs=in_specs, out_specs=grid, check_vma=False
    )
```

```python
import functools
import jax
import jax.numpy as jnp
import numpy as np
from jax import lax
from jax.experimental import pallas as pl
from jax.experimental.pallas import tpu as pltpu
from jax.sharding import Mesh, PartitionSpec as P

HEAD = 64
COUNT = 144
WIN_LEV = 2
WIN_LAT = 6
WIN_LON = 12
EPS = 1e-05
SCALE = 0.125
VMEM_LIMIT = 56 * 1024 * 1024
F32 = jnp.float32
BF16 = jnp.bfloat16


def normalize(values, gain):
    center = values - jnp.mean(values, -1, keepdims=True)
    spread = jnp.mean(center * center, -1, keepdims=True)
    return center * lax.rsqrt(spread + EPS) * gain


def dot(left, right):
    return jnp.dot(left, right, preferred_element_type=F32)


def gelu(x):
    return 0.5 * x * (1.0 + lax.erf(x * (0.5 ** 0.5)))


def fetch(order, buffers, place, semaphore):
    copies = []
    position = 0
    for buffer in buffers:
        for item in range(buffer.shape[0]):
            for source, target in place(buffer.at[item], order[position]):
                copies.append(pltpu.make_async_copy(source, target, semaphore))
            position += 1
    for copy in copies:
        copy.start()
    return copies


def await_all(copies):
    for copy in copies:
        copy.wait()


def attend_kernel(heads, start, masked, order, x_hbm, gain_ref, *rest):
    *buffers, out_ref, weights, x_ref, qkv, context, semaphore, x_semaphore = rest
    width = heads * HEAD
    share = width // 16
    tokens = x_ref.shape[0]
    x_copy = pltpu.make_async_copy(x_hbm.at[pl.ds(start, tokens)], x_ref, x_semaphore)
    x_copy.start()

    def place(block, index):
        rows = pl.ds(pl.multiple_of(index * share, share), share)
        return [(block, weights.at[rows, :])]

    copies = fetch(order, buffers, place, semaphore)
    x_copy.wait()
    normed = normalize(x_ref[...].astype(F32), gain_ref[...]).astype(BF16)
    await_all(copies)
    qkv[:, :width] = (dot(normed, weights[:, :width]) * SCALE).astype(BF16)
    qkv[:, width : 2 * width] = dot(normed, weights[:, width : 2 * width]).astype(BF16)
    qkv[:, 2 * width :] = dot(normed, weights[:, 2 * width : 3 * width]).astype(BF16)

    low = lax.broadcasted_iota(jnp.int32, (COUNT, 128), 1) < HEAD
    zero = jnp.zeros((COUNT, 128), BF16)
    one = jnp.ones((COUNT, 128), BF16)

    def late(shape, axis):
        token = lax.broadcasted_iota(jnp.int32, shape, axis)
        half = COUNT // 4
        return ((token >= half) & (token < 2 * half)) | (token >= 3 * half)

    def window(index, _):
        rows = pl.ds(pl.multiple_of(index * COUNT, COUNT), COUNT)
        if masked:
            apart = late((COUNT, COUNT), 0) != late((COUNT, COUNT), 1)
            wall = jnp.where(apart & (index > 0) & (order[16] > 0), -1e30, 0.0)
        for pair in range(heads // 2):
            lanes = slice(pair * 128, pair * 128 + 128)
            q = qkv[rows, lanes]
            k = qkv[rows, width + pair * 128 : width + pair * 128 + 128]
            v = qkv[rows, 2 * width + pair * 128 : 2 * width + pair * 128 + 128]
            results = []
            for half in range(2):
                mine = low if half == 0 else jnp.logical_not(low)
                scores = lax.dot_general(
                    q, jnp.where(mine, k, zero), (((1,), (1,)), ((), ())), preferred_element_type=F32
                )
                if masked:
                    scores = scores + wall
                powers = jnp.exp(scores - jnp.max(scores, -1, keepdims=True)).astype(BF16)
                results.append(dot(powers, jnp.where(mine, v, one)))
            upper = jnp.where(low, results[0], results[1])
            lower = jnp.where(low, results[1], results[0])
            context[rows, lanes] = (upper / pltpu.roll(lower, HEAD, 1)).astype(BF16)
        return 0

    lax.fori_loop(0, tokens // COUNT, window, 0)
    out_ref[...] = (x_ref[...].astype(F32) + dot(context[...], weights[:, 3 * width :])).astype(BF16)


def any_specs(buffers):
    return [pl.BlockSpec(memory_space=pl.ANY)] * len(buffers)


def attend(x, start, tokens, masked, gain, order, buffers, heads):
    width = x.shape[1]
    return pl.pallas_call(
        functools.partial(attend_kernel, heads, start, masked),
        out_shape=jax.ShapeDtypeStruct((tokens, width), BF16),
        in_specs=[
            pl.BlockSpec(memory_space=pltpu.SMEM),
            pl.BlockSpec(memory_space=pl.ANY),
            pl.BlockSpec(memory_space=pltpu.VMEM),
        ]
        + any_specs(buffers),
        out_specs=pl.BlockSpec(memory_space=pltpu.VMEM),
        scratch_shapes=[
            pltpu.VMEM((width, 4 * width), BF16),
            pltpu.VMEM((tokens, width), BF16),
            pltpu.VMEM((tokens, 3 * width), BF16),
            pltpu.VMEM((tokens, width), BF16),
            pltpu.SemaphoreType.DMA,
            pltpu.SemaphoreType.DMA,
        ],
        compiler_params=pltpu.CompilerParams(vmem_limit_bytes=VMEM_LIMIT),
        cost_estimate=pl.CostEstimate(
            flops=8 * tokens * width * width + 4 * tokens * COUNT * width,
            bytes_accessed=8 * width * width + 4 * tokens * width,
            transcendentals=tokens * COUNT * heads,
        ),
    )(order, x, gain.reshape(1, -1), *buffers)


def dense_kernel(edges, order, x_ref, gain_ref, *rest):
    if edges:
        *buffers, out_ref, south_ref, west_ref, corner_ref, expand, shrink, semaphore = rest
    else:
        *buffers, out_ref, expand, shrink, semaphore = rest
    tokens, width = x_ref.shape
    share = width // 16

    def place(block, index):
        rows = pl.ds(pl.multiple_of(index * share, share), share)
        pairs = [(block.at[:, : 4 * width], expand.at[rows, :])]
        for part in range(4):
            lanes = slice((4 + part) * width, (5 + part) * width)
            hidden_rows = pl.ds(pl.multiple_of((index * 4 + part) * share, share), share)
            pairs.append((block.at[:, lanes], shrink.at[hidden_rows, :]))
        return pairs

    copies = fetch(order, buffers, place, semaphore)
    x = x_ref[...].astype(F32)
    hidden = normalize(x, gain_ref[...]).astype(BF16)
    await_all(copies)
    total = x
    for part in range(4):
        lanes = slice(part * width, (part + 1) * width)
        grown = gelu(dot(hidden, expand[:, lanes])).astype(BF16)
        total = total + dot(grown, shrink[lanes, :])
    done = total.astype(BF16)
    out_ref[...] = done
    if edges:
        west_ref[:COUNT] = done[:COUNT]
        west_ref[COUNT:] = done[tokens - COUNT :]
        half = COUNT // 2
        target = lax.broadcasted_iota(jnp.int32, (half, COUNT), 0)
        source = lax.broadcasted_iota(jnp.int32, (half, COUNT), 1)
        quarter = half // 2
        chosen = (source == target + quarter + jnp.where(target >= quarter, quarter, 0)).astype(BF16)
        pieces = [
            dot(chosen, done[number * COUNT : number * COUNT + COUNT]) for number in range(tokens // COUNT)
        ]
        south_ref[...] = jnp.concatenate(pieces[1:], 0).astype(BF16)
        corner_ref[...] = pieces[-1].astype(BF16)


def dense(x, gain, order, buffers, edges):
    tokens, width = x.shape
    shapes = [x.shape]
    if edges:
        shapes += [(tokens // 2 - COUNT // 2, width), (2 * COUNT, width), (COUNT // 2, width)]
    return pl.pallas_call(
        functools.partial(dense_kernel, edges),
        out_shape=[jax.ShapeDtypeStruct(shape, BF16) for shape in shapes],
        in_specs=[
            pl.BlockSpec(memory_space=pltpu.SMEM),
            pl.BlockSpec(memory_space=pltpu.VMEM),
            pl.BlockSpec(memory_space=pltpu.VMEM),
        ]
        + any_specs(buffers),
        out_specs=[pl.BlockSpec(memory_space=pltpu.VMEM)] * len(shapes),
        scratch_shapes=[
            pltpu.VMEM((width, 4 * width), BF16),
            pltpu.VMEM((4 * width, width), BF16),
            pltpu.SemaphoreType.DMA,
        ],
        compiler_params=pltpu.CompilerParams(vmem_limit_bytes=VMEM_LIMIT),
        cost_estimate=pl.CostEstimate(
            flops=16 * tokens * width * width,
            bytes_accessed=16 * width * width + 4 * tokens * width,
            transcendentals=4 * tokens * width,
        ),
    )(order, x, gain.reshape(1, -1), *buffers)


def merge_kernel(
    order, upper_ref, lower_ref, south_ref, west_ref, corner_ref, pick_ref, south_pick_ref, corner_pick_ref, gain_ref, *rest
):
    *buffers, out_ref, weights, semaphore = rest
    width = upper_ref.shape[1]
    share = width // 4

    def place(block, index):
        rows = pl.ds(pl.multiple_of(index * share, share), share)
        return [(block, weights.at[rows, :])]

    copies = fetch(order, buffers, place, semaphore)

    def chosen(index, source):
        rows = lax.broadcasted_iota(jnp.int32, (index.shape[0], source.shape[0]), 1)
        return dot((rows == index).astype(BF16), source)

    def window(number):
        if number == -1:
            return west_ref[:COUNT], west_ref[COUNT:]
        rows = slice(number * COUNT, number * COUNT + COUNT)
        below = slice((number + 1) * COUNT, (number + 2) * COUNT)
        return lower_ref[:COUNT] if number == 5 else upper_ref[rows], lower_ref[below]

    results = []
    for coarse in range(3):
        sources = [part for number in (-1, 0, 1) for part in window(2 * coarse + number)]
        quad = chosen(pick_ref[...], jnp.concatenate(sources, 0))
        quad = quad + chosen(south_pick_ref[coarse], south_ref[...])
        if coarse == 0:
            quad = quad + chosen(corner_pick_ref[...], corner_ref[...])
        quarters = [quad[part * COUNT : part * COUNT + COUNT] for part in range(4)]
        mean = sum(jnp.sum(item, -1, keepdims=True) for item in quarters) / (4 * width)
        quarters = [item - mean for item in quarters]
        spread = sum(jnp.sum(item * item, -1, keepdims=True) for item in quarters) / (4 * width)
        level = lax.rsqrt(spread + EPS)
        results.append(
            [
                (item * level * gain_ref[:, part * width : part * width + width]).astype(BF16)
                for part, item in enumerate(quarters)
            ]
        )
    await_all(copies)
    total = None
    for part in range(4):
        normed = jnp.concatenate([item[part] for item in results], 0)
        term = dot(normed, weights[part * width : part * width + width, :])
        total = term if total is None else total + term
    out_ref[...] = total.astype(BF16)


def merge_picks():
    part, level, row, column = np.meshgrid(
        np.arange(4), np.arange(WIN_LEV), np.arange(WIN_LAT), np.arange(WIN_LON), indexing="ij"
    )
    part, level, row, column = (item.reshape(-1) for item in (part, level, row, column))
    fine_row = 2 * row + part % 2 - WIN_LAT // 2
    fine_column = 2 * column + part // 2 - WIN_LON // 2
    number = fine_column // WIN_LON
    column = fine_column % WIN_LON
    place = level * WIN_LAT * WIN_LON + (fine_row % WIN_LAT) * WIN_LON + column
    pick = np.where(fine_row >= 0, ((number + 1) * 2 + fine_row // WIN_LAT) * COUNT + place, -1)
    half = COUNT // 2
    place = level * half // 2 + (fine_row % WIN_LAT - WIN_LAT // 2) * WIN_LON + column
    south = []
    for coarse in range(3):
        window = 2 * coarse + number
        south.append(np.where((fine_row < 0) & (window >= 0), window * half + place, -1))
    corner = np.where((fine_row < 0) & (number < 0), place, -1)
    shape = (-1, 1)
    return [jnp.asarray(item.astype(np.int32)) for item in (pick.reshape(shape), np.stack(south)[:, :, None], corner.reshape(shape))]


def merge(upper, lower, south, west, corner, gain, order, buffers):
    width = upper.shape[1]
    tokens = 3 * COUNT
    return pl.pallas_call(
        merge_kernel,
        out_shape=jax.ShapeDtypeStruct((tokens, 2 * width), BF16),
        in_specs=[pl.BlockSpec(memory_space=pltpu.SMEM)]
        + [pl.BlockSpec(memory_space=pltpu.VMEM)] * 9
        + any_specs(buffers),
        out_specs=pl.BlockSpec(memory_space=pltpu.VMEM),
        scratch_shapes=[pltpu.VMEM((4 * width, 2 * width), BF16), pltpu.SemaphoreType.DMA],
        compiler_params=pltpu.CompilerParams(vmem_limit_bytes=VMEM_LIMIT),
        cost_estimate=pl.CostEstimate(
            flops=20 * tokens * width * width,
            bytes_accessed=16 * width * width + 12 * tokens * width,
            transcendentals=0,
        ),
    )(order, upper, lower, south, west, corner, *merge_picks(), gain.reshape(1, -1), *buffers)


def grow_kernel(order, x_ref, gain_ref, *rest):
    *buffers, out_ref, weights, semaphore = rest
    width = x_ref.shape[1]
    share = width // 16

    def place(block, index):
        rows = pl.ds(pl.multiple_of(index * share, share), share)
        return [(block, weights.at[rows, :])]

    copies = fetch(order, buffers, place, semaphore)
    hidden = normalize(x_ref[...].astype(F32), gain_ref[...]).astype(BF16)
    await_all(copies)
    for part in range(8):
        lanes = slice(part * (width // 2), (part + 1) * (width // 2))
        out_ref[:, lanes] = gelu(dot(hidden, weights[:, lanes])).astype(BF16)


def grow(x, gain, order, buffers):
    tokens, width = x.shape
    return pl.pallas_call(
        grow_kernel,
        out_shape=jax.ShapeDtypeStruct((tokens, 4 * width), BF16),
        in_specs=[
            pl.BlockSpec(memory_space=pltpu.SMEM),
            pl.BlockSpec(memory_space=pltpu.VMEM),
            pl.BlockSpec(memory_space=pltpu.VMEM),
        ]
        + any_specs(buffers),
        out_specs=pl.BlockSpec(memory_space=pltpu.VMEM),
        scratch_shapes=[pltpu.VMEM((width, 4 * width), BF16), pltpu.SemaphoreType.DMA],
        compiler_params=pltpu.CompilerParams(vmem_limit_bytes=VMEM_LIMIT),
        cost_estimate=pl.CostEstimate(
            flops=8 * tokens * width * width,
            bytes_accessed=8 * width * width + 10 * tokens * width,
            transcendentals=4 * tokens * width,
        ),
    )(order, x, gain.reshape(1, -1), *buffers)


def fold_kernel(order, x_ref, grown_ref, *rest):
    *buffers, out_ref, weights, semaphore = rest
    width = x_ref.shape[1]

    share = width // 4

    def place(block, index):
        rows = pl.ds(pl.multiple_of(index * share, share), share)
        return [(block, weights.at[rows, :])]

    await_all(fetch(order, buffers, place, semaphore))
    for half in range(2):
        lanes = slice(half * (width // 2), (half + 1) * (width // 2))
        back = dot(grown_ref[...], weights[:, lanes])
        out_ref[:, lanes] = (x_ref[:, lanes].astype(F32) + back).astype(BF16)


def fold(x, grown, order, buffers):
    tokens, width = x.shape
    return pl.pallas_call(
        fold_kernel,
        out_shape=jax.ShapeDtypeStruct((tokens, width), BF16),
        in_specs=[
            pl.BlockSpec(memory_space=pltpu.SMEM),
            pl.BlockSpec(memory_space=pltpu.VMEM),
            pl.BlockSpec(memory_space=pltpu.VMEM),
        ]
        + any_specs(buffers),
        out_specs=pl.BlockSpec(memory_space=pltpu.VMEM),
        scratch_shapes=[pltpu.VMEM((4 * width, width), BF16), pltpu.SemaphoreType.DMA],
        compiler_params=pltpu.CompilerParams(vmem_limit_bytes=VMEM_LIMIT),
        cost_estimate=pl.CostEstimate(
            flops=8 * tokens * width * width,
            bytes_accessed=8 * width * width + 12 * tokens * width,
            transcendentals=0,
        ),
    )(order, x, grown, *buffers)


LAT = ("x", "zh")
LON = ("y", "zl", "c")


def gather(shard):
    return [lax.all_gather(shard, LON, axis=0, tiled=False)]


def tie(values, *others):
    return lax.optimization_barrier((values, others))[0]


def step_y(block, steps):
    return lax.ppermute(block, "y", [(place, (place + steps) % 4) for place in range(4)])


def step_z(block, steps):
    return lax.ppermute(block, ("zh", "zl"), [(place, (place + steps) % 4) for place in range(4)])


def step_core(block):
    return lax.ppermute(block, "c", [(0, 1), (1, 0)])


def step_diagonal(block, steps):
    pairs = [(lat * 16 + lon, (lat + steps) % 8 * 16 + (lon + steps) % 16) for lat in range(8) for lon in range(16)]
    return lax.ppermute(block, LAT + LON, pairs)


def spread_order():
    y, zl, c = (lax.axis_index(name) for name in LON)
    places = []
    for other_core in range(2):
        for other_z in range(2):
            for steps in (0, 2, 3, 1):
                places.append(((y + steps) % 4) * 4 + (zl ^ other_z) * 2 + (c ^ other_core))
    return jnp.stack(places).astype(jnp.int32)


def spread_y(shard):
    return [shard[None], step_y(shard, 2)[None], step_y(shard, 1)[None], step_y(shard, -1)[None]]


def paired(near):
    return [jnp.concatenate(near[:2]), jnp.concatenate(near[2:])]


def spread_z(pairs):
    return [step_z(pairs[0], 1), step_z(pairs[1], -1)]


def spread_core(pairs):
    return [step_core(block) for block in pairs]


def fence(*values):
    return lax.optimization_barrier(values)


def passed_along(value, axes, steps):
    count = 1
    for axis in axes:
        count *= lax.axis_size(axis)
    pairs = [(source, (source + steps) % count) for source in range(count)]
    return lax.ppermute(value, axes, pairs)


def window_split(grid):
    levels, rows, cols, width = grid.shape
    parts = grid.reshape(levels, rows // WIN_LAT, WIN_LAT, cols // WIN_LON, WIN_LON, width)
    return parts.transpose(1, 3, 0, 2, 4, 5).reshape(-1, width)


def window_join(parts, rows, cols):
    width = parts.shape[-1]
    grid = parts.reshape(rows // WIN_LAT, cols // WIN_LON, WIN_LEV, WIN_LAT, WIN_LON, width)
    return grid.transpose(2, 0, 3, 1, 4, 5).reshape(WIN_LEV, rows, cols, width)


def in_lanes(shard, parts):
    return [shard[part * shard.shape[0] // parts : (part + 1) * shard.shape[0] // parts] for part in range(parts)]


def per_device(
    latents,
    attend_gain,
    packed_heads,
    heads_back,
    dense_gain,
    expand_weight,
    shrink_weight,
    merge_gain,
    merge_weight,
    coarse_gain,
    coarse_heads,
    coarse_back,
    coarse_scale,
    coarse_expand,
    coarse_shrink,
):
    _, rows, cols, width = latents.shape
    order = jnp.arange(16, dtype=jnp.int32)
    place = lax.axis_index("x") * 2 + lax.axis_index("zh")
    last = (place == lax.axis_size("x") * 2 - 1).astype(jnp.int32)
    places = jnp.concatenate([spread_order(), last[None]])
    first = jnp.concatenate([packed_heads, heads_back], 1)
    second = jnp.concatenate([expand_weight] + in_lanes(shrink_weight, 4), 1)
    third = merge_weight
    coarse_attend = gather(jnp.concatenate([coarse_heads, coarse_back], 1))
    coarse_grow = gather(coarse_expand)
    lat_cut, lon_cut = WIN_LAT // 2, WIN_LON // 2

    near = spread_y(first)
    south_edge = passed_along(latents[:, :lat_cut], LAT, -1)
    east_edge = passed_along(latents[:, :, :lon_cut], LON, -1)
    near, east_edge = fence(near, east_edge)
    a_near = paired(near)
    a_far = spread_z(a_near)
    a_mate = spread_core(a_near)
    a_near, a_far, a_mate, south_edge = fence(a_near, a_far, a_mate, south_edge)
    a_mate += spread_core(a_far)
    corner = step_diagonal(latents[:, :lat_cut, :lon_cut], -1)
    near = spread_y(tie(second, a_near))
    rolled = jnp.concatenate(
        [
            jnp.concatenate([latents[:, lat_cut:, lon_cut:], east_edge[:, lat_cut:]], 2),
            jnp.concatenate([south_edge[:, :, lon_cut:], corner], 2),
        ],
        1,
    )
    windows = window_split(rolled)
    fine_attend = a_near + a_far + a_mate

    lower = attend(windows, 5 * COUNT, 7 * COUNT, True, attend_gain, places, fine_attend, 8)
    near, lower, windows = fence(near, lower, windows)
    b_near = paired(near)
    b_far = spread_z(b_near)
    near = spread_y(tie(third, lower))
    upper = attend(windows, 0, 5 * COUNT, False, attend_gain, places, fine_attend, 8)
    near, b_near, b_far, upper = fence(near, b_near, b_far, upper)
    b_mate = spread_core(b_near) + spread_core(b_far)
    b_mate, near = fence(b_mate, near)
    c_near = paired(near)
    c_far = spread_z(c_near)
    c_mate = spread_core(c_near)

    fine_dense = b_near + b_far + b_mate
    lower, south, west, corner = dense(tie(lower, c_near), dense_gain, places, fine_dense, True)
    c_near, c_far, c_mate, lower, south, west, corner = fence(c_near, c_far, c_mate, lower, south, west, corner)
    south = passed_along(south, LAT, 1)
    west = passed_along(west, LON, 1)
    corner = step_diagonal(corner, 1)
    c_mate += spread_core(c_far)
    (upper,) = dense(tie(upper, lower), dense_gain, places, fine_dense, False)
    upper, south, west, corner, c_mate = fence(upper, south, west, corner, c_mate)
    near = spread_y(tie(coarse_shrink, upper))
    merging = c_near + c_far + c_mate
    merged = merge(upper, lower, south, west, corner, merge_gain, places, merging)
    coarse_mixed = attend(merged, 0, 3 * COUNT, False, coarse_gain, order, coarse_attend, 16)
    near, coarse_mixed = fence(near, coarse_mixed)
    d_near = paired(near)
    d_far = spread_z(d_near)
    d_mate = spread_core(d_near)
    grown = grow(coarse_mixed, coarse_scale, order, coarse_grow)
    d_far, d_mate, grown = fence(d_far, d_mate, grown)
    d_mate += spread_core(d_far)
    finished = fold(coarse_mixed, grown, places, d_near + d_far + d_mate)
    return window_join(finished, rows // 2, cols // 2)


def solution(mesh):
    fine_mesh = Mesh(mesh.devices.reshape(4, 2, 4, 2, 2), ("x", "zh", "y", "zl", "c"))
    rows = P(LON, None)
    grid = P(None, LAT, LON, None)
    in_specs = (grid, P(), rows, rows, P(), rows, rows, P(), rows, P(), rows, rows, P(), rows, rows)
    return jax.shard_map(
        per_device, mesh=fine_mesh, in_specs=in_specs, out_specs=grid, check_vma=False
    )
```

```python
import functools
import jax
import jax.numpy as jnp
import numpy as np
from jax import lax
from jax.experimental import pallas as pl
from jax.experimental.pallas import tpu as pltpu
from jax.sharding import Mesh, PartitionSpec as P

HEAD = 64
COUNT = 144
WIN_LEV = 2
WIN_LAT = 6
WIN_LON = 12
EPS = 1e-05
SCALE = 0.125
VMEM_LIMIT = 56 * 1024 * 1024
F32 = jnp.float32
BF16 = jnp.bfloat16


def normalize(values, gain):
    center = values - jnp.mean(values, -1, keepdims=True)
    spread = jnp.mean(center * center, -1, keepdims=True)
    return center * lax.rsqrt(spread + EPS) * gain


def dot(left, right):
    return jnp.dot(left, right, preferred_element_type=F32)


def gelu(x):
    return 0.5 * x * (1.0 + lax.erf(x * (0.5 ** 0.5)))


def fetch(order, buffers, place, semaphore):
    copies = []
    position = 0
    for buffer in buffers:
        for item in range(buffer.shape[0]):
            for source, target in place(buffer.at[item], order[position]):
                copies.append(pltpu.make_async_copy(source, target, semaphore))
            position += 1
    for copy in copies:
        copy.start()
    return copies


def await_all(copies):
    for copy in copies:
        copy.wait()


def fetch_quarters(order, gathered, first, place, semaphore):
    copies = []
    for position in range(gathered.shape[0]):
        for other in range(2):
            source = gathered.at[position, other, pl.ds(first, 4)]
            copies.append(pltpu.make_async_copy(source, place(order[2 * position + other]), semaphore))
    for copy in copies:
        copy.start()
    return copies


def attend_windows(qkv, context, heads, wall_of):
    width = heads * HEAD
    low = lax.broadcasted_iota(jnp.int32, (COUNT, 128), 1) < HEAD
    zero = jnp.zeros((COUNT, 128), BF16)
    one = jnp.ones((COUNT, 128), BF16)

    def window(index, _):
        rows = pl.ds(pl.multiple_of(index * COUNT, COUNT), COUNT)
        wall = wall_of(index)
        for pair in range(heads // 2):
            lanes = slice(pair * 128, pair * 128 + 128)
            q = qkv[rows, lanes]
            k = qkv[rows, width + pair * 128 : width + pair * 128 + 128]
            v = qkv[rows, 2 * width + pair * 128 : 2 * width + pair * 128 + 128]
            results = []
            for half in range(2):
                mine = low if half == 0 else jnp.logical_not(low)
                scores = lax.dot_general(
                    q, jnp.where(mine, k, zero), (((1,), (1,)), ((), ())), preferred_element_type=F32
                )
                if wall is not None:
                    scores = scores + wall
                powers = jnp.exp(scores - jnp.max(scores, -1, keepdims=True)).astype(BF16)
                results.append(dot(powers, jnp.where(mine, v, one)))
            upper = jnp.where(low, results[0], results[1])
            lower = jnp.where(low, results[1], results[0])
            context[rows, lanes] = (upper / pltpu.roll(lower, HEAD, 1)).astype(BF16)
        return 0

    lax.fori_loop(0, context.shape[0] // COUNT, window, 0)


def late(shape, axis):
    return lax.broadcasted_iota(jnp.int32, shape, axis) >= COUNT // 2


def attend_kernel(lowest, order, grid_ref, *rest):
    if lowest:
        south_ref, east_ref, gain_ref, *buffers, edge_ref, out_ref, weights, x, qkv, context, semaphore = rest
    else:
        gain_ref, *buffers, out_ref, weights, x, qkv, context, semaphore = rest
    tokens, width = x.shape
    share = width // 16
    lat_cut, lon_cut = WIN_LAT // 2, WIN_LON // 2
    columns = grid_ref.shape[2]

    def place(block, index):
        rows = pl.ds(pl.multiple_of(index * share, share), share)
        return [(block, weights.at[rows, :])]

    copies = fetch(order, buffers, place, semaphore)
    across = columns // WIN_LON
    windows = [(0, number) for number in range(across - 1)]
    if lowest:
        windows = [(0, across - 1)] + [(1, number) for number in range(across)]
    for position, (band, number) in enumerate(windows):
        for level in range(WIN_LEV):
            for row in range(WIN_LAT):
                rolled = band * WIN_LAT + row
                target = position * COUNT + (row * WIN_LEV + level) * WIN_LON
                first = number * WIN_LON + lon_cut
                count = min(WIN_LON, columns - first)
                if rolled + lat_cut < grid_ref.shape[1]:
                    piece = grid_ref[level, rolled + lat_cut, first : first + count, :]
                else:
                    piece = south_ref[level, rolled + lat_cut - grid_ref.shape[1], first : first + count, :]
                x[target : target + count, :] = piece.astype(F32)
                if count < WIN_LON:
                    x[target + count : target + WIN_LON, :] = east_ref[level, rolled, :, :].astype(F32)

    normed = normalize(x[...], gain_ref[...]).astype(BF16)
    await_all(copies)
    qkv[:, :width] = (dot(normed, weights[:, :width]) * SCALE).astype(BF16)
    qkv[:, width:] = dot(normed, weights[:, width : 3 * width]).astype(BF16)

    def wall_of(index):
        if not lowest:
            return None
        apart = late((COUNT, COUNT), 0) != late((COUNT, COUNT), 1)
        return jnp.where(apart & (index > 0) & (order[16] > 0), -1e30, 0.0)

    attend_windows(qkv, context, width // HEAD, wall_of)
    done = x[...] + dot(context[...], weights[:, 3 * width :])
    if lowest:
        half = COUNT // 2
        starts = range(COUNT, tokens, COUNT)
        edge = [done[start + half : start + COUNT] for start in starts] + [done[:COUNT], done[tokens - COUNT : tokens - half]]
        edge_ref[...] = jnp.concatenate(edge, 0).astype(BF16)
        out_ref[...] = jnp.concatenate([done[start : start + half] for start in starts[:-1]], 0).astype(BF16)
    else:
        out_ref[...] = done.astype(BF16)


def any_specs(buffers):
    return [pl.BlockSpec(memory_space=pl.ANY)] * len(buffers)


def attend(grid, edges, gain, order, buffers):
    width = grid.shape[-1]
    across = grid.shape[2] // WIN_LON
    tokens = (across + 1 if edges else across - 1) * COUNT
    rest = tokens if not edges else (across - 1) * COUNT // 2
    shapes = [(tokens - rest, width), (rest, width)] if edges else [(rest, width)]
    return pl.pallas_call(
        functools.partial(attend_kernel, bool(edges)),
        out_shape=[jax.ShapeDtypeStruct(shape, BF16) for shape in shapes],
        in_specs=[pl.BlockSpec(memory_space=pltpu.SMEM)]
        + [pl.BlockSpec(memory_space=pltpu.VMEM)] * (2 + len(edges))
        + any_specs(buffers),
        out_specs=[pl.BlockSpec(memory_space=pltpu.VMEM)] * len(shapes),
        scratch_shapes=[
            pltpu.VMEM((width, 4 * width), BF16),
            pltpu.VMEM((tokens, width), F32),
            pltpu.VMEM((tokens, 3 * width), BF16),
            pltpu.VMEM((tokens, width), BF16),
            pltpu.SemaphoreType.DMA,
        ],
        compiler_params=pltpu.CompilerParams(vmem_limit_bytes=VMEM_LIMIT),
        cost_estimate=pl.CostEstimate(
            flops=8 * tokens * width * width + 4 * tokens * COUNT * width,
            bytes_accessed=8 * width * width + 4 * tokens * width,
            transcendentals=tokens * COUNT * (width // HEAD),
        ),
    )(order, grid, *edges, gain.reshape(1, -1), *buffers)


def dense_kernel(parts, edges, order, *rest):
    inputs, (gain_ref, *buffers), outs = rest[:parts], rest[parts : parts + 9], rest[parts + 9 : -3]
    expand, shrink, semaphore = rest[-3:]
    width = gain_ref.shape[1]
    share = width // 16

    def place(block, index):
        rows = pl.ds(pl.multiple_of(index * share, share), share)
        pairs = [(block.at[:, : 4 * width], expand.at[rows, :])]
        for part in range(4):
            lanes = slice((4 + part) * width, (5 + part) * width)
            hidden_rows = pl.ds(pl.multiple_of((index * 4 + part) * share, share), share)
            pairs.append((block.at[:, lanes], shrink.at[hidden_rows, :]))
        return pairs

    copies = fetch(order, buffers, place, semaphore)
    x = jnp.concatenate([ref[...].astype(F32) for ref in inputs], 0)
    hidden = normalize(x, gain_ref[...]).astype(BF16)
    await_all(copies)
    total = x
    for part in range(4):
        lanes = slice(part * width, (part + 1) * width)
        grown = gelu(dot(hidden, expand[:, lanes])).astype(BF16)
        total = total + dot(grown, shrink[lanes, :])
    start = 0
    for ref in outs[:2] if edges else outs:
        ref[...] = total[start : start + ref.shape[0]].astype(BF16)
        start += ref.shape[0]
    if edges:
        south_ref, _, corner_ref = outs
        last = south_ref.shape[0]
        corner_ref[...] = total[last - corner_ref.shape[0] : last].astype(BF16)


def dense(inputs, gain, order, buffers, edges):
    width = inputs[0].shape[1]
    tokens = sum(item.shape[0] for item in inputs)
    half = COUNT // 2
    shapes = [(tokens - 3 * half, width), (3 * half, width), (half, width)] if edges else [item.shape for item in inputs]
    return pl.pallas_call(
        functools.partial(dense_kernel, len(inputs), edges),
        out_shape=[jax.ShapeDtypeStruct(shape, BF16) for shape in shapes],
        in_specs=[pl.BlockSpec(memory_space=pltpu.SMEM)]
        + [pl.BlockSpec(memory_space=pltpu.VMEM)] * (len(inputs) + 1)
        + any_specs(buffers),
        out_specs=[pl.BlockSpec(memory_space=pltpu.VMEM)] * len(shapes),
        scratch_shapes=[
            pltpu.VMEM((width, 4 * width), BF16),
            pltpu.VMEM((4 * width, width), BF16),
            pltpu.SemaphoreType.DMA,
        ],
        compiler_params=pltpu.CompilerParams(vmem_limit_bytes=VMEM_LIMIT),
        cost_estimate=pl.CostEstimate(
            flops=16 * tokens * width * width,
            bytes_accessed=16 * width * width + 4 * tokens * width,
            transcendentals=4 * tokens * width,
        ),
    )(order, *inputs, gain.reshape(1, -1), *buffers)


def merge_kernel(order, *rest):
    upper_ref, lower_ref, side_ref, south_ref, west_ref, corner_ref = rest[:6]
    pick_ref, south_pick_ref, corner_pick_ref, gain_ref, *buffers, out_ref, weights, semaphore = rest[6:]
    width = upper_ref.shape[1]
    share = width // 4
    half = COUNT // 2

    def place(block, index):
        rows = pl.ds(pl.multiple_of(index * share, share), share)
        return [(block, weights.at[rows, :])]

    copies = fetch(order, buffers, place, semaphore)

    def chosen(index, source):
        rows = lax.broadcasted_iota(jnp.int32, (index.shape[0], source.shape[0]), 1)
        return dot((rows == index).astype(BF16), source)

    def window(number):
        if number in (-1, 5):
            ref = west_ref if number < 0 else side_ref
            return ref[:COUNT], ref[COUNT:]
        return upper_ref[number * COUNT : number * COUNT + COUNT], lower_ref[number * half : number * half + half]

    results = []
    for coarse in range(3):
        sources = [window(2 * coarse + number) for number in (-1, 0, 1)]
        sources = [item[0] for item in sources] + [item[1] for item in sources]
        quad = chosen(pick_ref[...], jnp.concatenate(sources, 0))
        quad = quad + chosen(south_pick_ref[coarse], south_ref[...])
        if coarse == 0:
            quad = quad + chosen(corner_pick_ref[...], corner_ref[...])
        quarters = [quad[part * COUNT : part * COUNT + COUNT] for part in range(4)]
        mean = sum(jnp.sum(item, -1, keepdims=True) for item in quarters) / (4 * width)
        quarters = [item - mean for item in quarters]
        spread = sum(jnp.sum(item * item, -1, keepdims=True) for item in quarters) / (4 * width)
        level = lax.rsqrt(spread + EPS)
        results.append(
            [
                (item * level * gain_ref[:, part * width : part * width + width]).astype(BF16)
                for part, item in enumerate(quarters)
            ]
        )
    await_all(copies)
    total = None
    for part in range(4):
        normed = jnp.concatenate([item[part] for item in results], 0)
        term = dot(normed, weights[part * width : part * width + width, :])
        total = term if total is None else total + term
    out_ref[...] = total.astype(BF16)


def merge_picks():
    part, level, row, column = np.meshgrid(
        np.arange(4), np.arange(WIN_LEV), np.arange(WIN_LAT), np.arange(WIN_LON), indexing="ij"
    )
    part, level, row, column = (item.reshape(-1) for item in (part, level, row, column))
    fine_row = 2 * row + part % 2 - WIN_LAT // 2
    fine_column = 2 * column + part // 2 - WIN_LON // 2
    number = fine_column // WIN_LON
    column = fine_column % WIN_LON
    half = COUNT // 2
    place = ((fine_row % WIN_LAT) * WIN_LEV + level) * WIN_LON + column
    pick = np.where(fine_row < WIN_LAT, (number + 1) * COUNT, 3 * COUNT + (number + 1) * half) + place
    pick = np.where(fine_row >= 0, pick, -1)
    place = place - half
    south = []
    for coarse in range(3):
        window = 2 * coarse + number
        south.append(np.where((fine_row < 0) & (window >= 0), window * half + place, -1))
    corner = np.where((fine_row < 0) & (number < 0), place, -1)
    shape = (-1, 1)
    return [jnp.asarray(item.astype(np.int32)) for item in (pick.reshape(shape), np.stack(south)[:, :, None], corner.reshape(shape))]


def merge(sources, gain, order, buffers):
    width = sources[0].shape[1]
    tokens = 3 * COUNT
    return pl.pallas_call(
        merge_kernel,
        out_shape=jax.ShapeDtypeStruct((tokens, 2 * width), BF16),
        in_specs=[pl.BlockSpec(memory_space=pltpu.SMEM)]
        + [pl.BlockSpec(memory_space=pltpu.VMEM)] * 10
        + any_specs(buffers),
        out_specs=pl.BlockSpec(memory_space=pltpu.VMEM),
        scratch_shapes=[pltpu.VMEM((4 * width, 2 * width), BF16), pltpu.SemaphoreType.DMA],
        compiler_params=pltpu.CompilerParams(vmem_limit_bytes=VMEM_LIMIT),
        cost_estimate=pl.CostEstimate(
            flops=20 * tokens * width * width,
            bytes_accessed=16 * width * width + 12 * tokens * width,
            transcendentals=0,
        ),
    )(order, *sources, *merge_picks(), gain.reshape(1, -1), *buffers)


def coarse_kernel(order, x_ref, attend_gain_ref, dense_gain_ref, gathered, out_ref, *scratch):
    weights, expand, shrink, qkv, context, mixed, grown, semaphores = scratch
    tokens, width = x_ref.shape
    half = width // 2

    def rows_of(target):
        return lambda index: target.at[:, pl.ds(pl.multiple_of(index * 16, 16), 16), :]

    attend_copies = fetch_quarters(order, gathered, 0, rows_of(weights), semaphores.at[0])
    expand_copies = fetch_quarters(order, gathered, 4, rows_of(expand), semaphores.at[1])
    shrink_copies = fetch_quarters(order, gathered, 8, lambda index: shrink.at[pl.ds(index * 4, 4)], semaphores.at[2])

    normed = normalize(x_ref[...].astype(F32), attend_gain_ref[...]).astype(BF16)
    await_all(attend_copies)
    qkv[:, :width] = (dot(normed, weights[0]) * SCALE).astype(BF16)
    qkv[:, width : 2 * width] = dot(normed, weights[1]).astype(BF16)
    qkv[:, 2 * width :] = dot(normed, weights[2]).astype(BF16)
    attend_windows(qkv, context, width // HEAD, lambda index: None)
    mixed[...] = (x_ref[...].astype(F32) + dot(context[...], weights[3])).astype(BF16)

    hidden = normalize(mixed[...].astype(F32), dense_gain_ref[...]).astype(BF16)
    await_all(expand_copies)
    for part in range(8):
        lanes = slice(part % 2 * half, (part % 2 + 1) * half)
        grown[:, part * half : part * half + half] = gelu(dot(hidden, expand[part // 2, :, lanes])).astype(BF16)
    await_all(shrink_copies)
    for part in range(2):
        lanes = slice(part * half, part * half + half)
        back = dot(grown[...], shrink[:, :, lanes].reshape(4 * width, half))
        out_ref[:, lanes] = (mixed[:, lanes].astype(F32) + back).astype(BF16)


def coarse(x, attend_gain, dense_gain, order, gathered):
    tokens, width = x.shape
    return pl.pallas_call(
        coarse_kernel,
        out_shape=jax.ShapeDtypeStruct((tokens, width), BF16),
        in_specs=[pl.BlockSpec(memory_space=pltpu.SMEM)]
        + [pl.BlockSpec(memory_space=pltpu.VMEM)] * 3
        + [pl.BlockSpec(memory_space=pl.ANY)],
        out_specs=pl.BlockSpec(memory_space=pltpu.VMEM),
        scratch_shapes=[
            pltpu.VMEM((4, width, width), BF16),
            pltpu.VMEM((4, width, width), BF16),
            pltpu.VMEM((4 * width // 16, 16, width), BF16),
            pltpu.VMEM((tokens, 3 * width), BF16),
            pltpu.VMEM((tokens, width), BF16),
            pltpu.VMEM((tokens, width), BF16),
            pltpu.VMEM((tokens, 4 * width), BF16),
            pltpu.SemaphoreType.DMA((3,)),
        ],
        compiler_params=pltpu.CompilerParams(vmem_limit_bytes=VMEM_LIMIT),
        cost_estimate=pl.CostEstimate(
            flops=24 * tokens * width * width + 4 * tokens * COUNT * width,
            bytes_accessed=24 * width * width + 4 * tokens * width,
            transcendentals=4 * tokens * width,
        ),
    )(order, x, attend_gain.reshape(1, -1), dense_gain.reshape(1, -1), gathered)


def pack_kernel(place, heads, back, expand, shrink, wide_heads, wide_back, wide_expand, wide_shrink, *outs):
    first, second, mine, pair = outs
    rows, width = back.shape
    wide = wide_back.shape[1]
    own = pl.ds(pl.multiple_of(place[0] * 16, 16), 16)
    first[:, : 3 * width] = heads[...]
    first[:, 3 * width :] = back[...]
    second[:, : 4 * width] = expand[...]
    for part in range(4):
        second[:, (4 + part) * width : (5 + part) * width] = shrink[part * rows : (part + 1) * rows, :]
    for part in range(3):
        mine[part] = wide_heads[own, part * wide : (part + 1) * wide]
    mine[3] = wide_back[own, :]
    for part in range(4):
        mine[4 + part] = wide_expand[own, part * wide : (part + 1) * wide]
        start = pl.multiple_of(place[0] * 64 + part * 16, 16)
        mine[8 + part] = wide_shrink[pl.ds(start, 16), :]
    pair[0] = mine[...]


def pack(place, *shards):
    rows, width = shards[1].shape
    wide = shards[5].shape[1]
    shapes = [(rows, 4 * width), (rows, 8 * width), (12, 16, wide), (2, 12, 16, wide)]
    return pl.pallas_call(
        pack_kernel,
        out_shape=[jax.ShapeDtypeStruct(shape, BF16) for shape in shapes],
        in_specs=[pl.BlockSpec(memory_space=pltpu.SMEM)] + [pl.BlockSpec(memory_space=pltpu.VMEM)] * len(shards),
        out_specs=[pl.BlockSpec(memory_space=pltpu.VMEM)] * 4,
        compiler_params=pltpu.CompilerParams(vmem_limit_bytes=VMEM_LIMIT),
    )(place, *shards)


LAT = ("x", "zh")
LON = ("y", "zl", "c")


def tie(values, *others):
    return lax.optimization_barrier((values, others))[0]


def step_y(block, steps):
    return lax.ppermute(block, "y", [(place, (place + steps) % 4) for place in range(4)])


def step_z(block, steps):
    return lax.ppermute(block, ("zh", "zl"), [(place, (place + steps) % 4) for place in range(4)])


def step_core(block):
    return lax.ppermute(block, "c", [(0, 1), (1, 0)])


def step_diagonal(block, steps):
    pairs = [(lat * 16 + lon, (lat + steps) % 8 * 16 + (lon + steps) % 16) for lat in range(8) for lon in range(16)]
    return lax.ppermute(block, LAT + LON, pairs)


def spread_order():
    y, zl, c = (lax.axis_index(name) for name in LON)
    places = []
    for other_core in range(2):
        for other_z in range(2):
            for steps in (0, 2, 3, 1):
                places.append(((y + steps) % 4) * 4 + (zl ^ other_z) * 2 + (c ^ other_core))
    return jnp.stack(places).astype(jnp.int32)


def quarter_order():
    zl = lax.axis_index("zl")
    x, y, c, other = jnp.meshgrid(jnp.arange(4), jnp.arange(4), jnp.arange(2), jnp.arange(2), indexing="ij")
    block = y * 4 + (zl ^ other) * 2 + c
    return (block * 4 + x).reshape(-1).astype(jnp.int32)


def spread_y(shard):
    return [shard[None], step_y(shard, 2)[None], step_y(shard, 1)[None], step_y(shard, -1)[None]]


def paired(near):
    return [jnp.concatenate(near[:2]), jnp.concatenate(near[2:])]


def spread_z(pairs):
    return [step_z(pairs[0], 1), step_z(pairs[1], -1)]


def spread_core(pairs):
    return [step_core(block) for block in pairs]


def fence(*values):
    return lax.optimization_barrier(values)


def passed_along(value, axes, steps):
    count = 1
    for axis in axes:
        count *= lax.axis_size(axis)
    pairs = [(source, (source + steps) % count) for source in range(count)]
    return lax.ppermute(value, axes, pairs)


def per_device(
    latents,
    attend_gain,
    packed_heads,
    heads_back,
    dense_gain,
    expand_weight,
    shrink_weight,
    merge_gain,
    merge_weight,
    coarse_gain,
    coarse_heads,
    coarse_back,
    coarse_scale,
    coarse_expand,
    coarse_shrink,
):
    lat_cut, lon_cut = WIN_LAT // 2, WIN_LON // 2
    order = quarter_order()
    place = lax.axis_index("x") * 2 + lax.axis_index("zh")
    last = (place == lax.axis_size("x") * 2 - 1).astype(jnp.int32)
    places = jnp.concatenate([spread_order(), last[None]])

    first, second, mine, pair = pack(
        lax.axis_index("x")[None].astype(jnp.int32),
        packed_heads,
        heads_back,
        expand_weight,
        shrink_weight,
        coarse_heads,
        coarse_back,
        coarse_expand,
        coarse_shrink,
    )
    other = step_z(mine, 1)
    near = spread_y(first)
    near, pair, other = fence(near, pair, other)
    gathered = lax.all_gather(pair.at[1].set(other), ("x", "y", "c"), axis=0, tiled=False)
    a_near = paired(near)
    a_far = spread_z(a_near)
    a_mate = spread_core(a_near)
    east_edge = passed_along(tie(latents[:, lat_cut:, :lon_cut], a_near), LON, -1)
    a_near, a_far, a_mate, east_edge = fence(a_near, a_far, a_mate, east_edge)
    a_mate += spread_core(a_far)
    south_edge = passed_along(tie(latents[:, :lat_cut], a_near), LAT, -1)
    corner = step_diagonal(tie(latents[:, :lat_cut, :lon_cut], a_near), -1)
    near = spread_y(tie(second, a_mate))
    fine_attend = a_near + a_far + a_mate

    (upper,) = attend(latents, [], attend_gain, places, fine_attend)
    near, upper, south_edge, corner = fence(near, upper, south_edge, corner)
    east_edge = jnp.concatenate([east_edge, corner], 1)
    b_near = paired(near)
    b_far = spread_z(b_near)
    near = spread_y(tie(merge_weight, upper))
    edge, lower = attend(tie(latents, upper), [south_edge, east_edge], attend_gain, places, fine_attend)
    near, b_near, b_far, edge, lower = fence(near, b_near, b_far, edge, lower)
    b_mate = spread_core(b_near) + spread_core(b_far)
    b_mate, near = fence(b_mate, near)
    c_near = paired(near)
    c_far = spread_z(c_near)
    c_mate = spread_core(c_near)

    fine_dense = b_near + b_far + b_mate
    south, side, corner = dense([tie(edge, c_near)], dense_gain, places, fine_dense, True)
    c_near, c_mate, south, side, corner = fence(c_near, c_mate, south, side, corner)
    south = passed_along(south, LAT, 1)
    west = passed_along(side, LON, 1)
    corner = step_diagonal(corner, 1)
    upper, lower = dense(tie([upper, lower], side), dense_gain, places, fine_dense, False)
    upper, lower, c_far, south, west, corner = fence(upper, lower, c_far, south, west, corner)
    merging = c_near + c_far + c_mate + spread_core(c_far)
    merged = merge([upper, lower, side, south, west, corner], merge_gain, places, merging)
    finished = coarse(merged, coarse_gain, coarse_scale, order, gathered)
    grid = finished.reshape(3, WIN_LEV, WIN_LAT, WIN_LON, -1).transpose(1, 2, 0, 3, 4)
    return grid.reshape(WIN_LEV, WIN_LAT, 3 * WIN_LON, -1)


def solution(mesh):
    fine_mesh = Mesh(mesh.devices.reshape(4, 2, 4, 2, 2), ("x", "zh", "y", "zl", "c"))
    rows = P(LON, None)
    grid = P(None, LAT, LON, None)
    in_specs = (grid, P(), rows, rows, P(), rows, rows, P(), rows, P(), rows, rows, P(), rows, rows)
    return jax.shard_map(
        per_device, mesh=fine_mesh, in_specs=in_specs, out_specs=grid, check_vma=False
    )
```

```python
import functools
import jax
import jax.numpy as jnp
import numpy as np
from jax import lax
from jax.experimental import pallas as pl
from jax.experimental.pallas import tpu as pltpu
from jax.sharding import Mesh, PartitionSpec as P

HEAD = 64
COUNT = 144
WIN_LEV = 2
WIN_LAT = 6
WIN_LON = 12
EPS = 1e-05
SCALE = 0.125
VMEM_LIMIT = 56 * 1024 * 1024
F32 = jnp.float32
BF16 = jnp.bfloat16


def normalize(values, gain):
    center = values - jnp.mean(values, -1, keepdims=True)
    spread = jnp.mean(center * center, -1, keepdims=True)
    return center * lax.rsqrt(spread + EPS) * gain


def dot(left, right):
    return jnp.dot(left, right, preferred_element_type=F32)


def gelu(x):
    return 0.5 * x * (1.0 + lax.erf(x * (0.5 ** 0.5)))


def fetch(order, buffers, place, semaphore):
    copies = []
    position = 0
    for buffer in buffers:
        for item in range(buffer.shape[0]):
            for source, target in place(buffer.at[item], order[position]):
                copies.append(pltpu.make_async_copy(source, target, semaphore))
            position += 1
    for copy in copies:
        copy.start()
    return copies


def await_all(copies):
    for copy in copies:
        copy.wait()


def fetch_quarters(order, gathered, first, place, semaphore):
    copies = []
    for position in range(gathered.shape[0]):
        for other in range(2):
            source = gathered.at[position, other, pl.ds(first, 4)]
            copies.append(pltpu.make_async_copy(source, place(order[2 * position + other]), semaphore))
    for copy in copies:
        copy.start()
    return copies


def attend_windows(qkv, context, heads, wall_of):
    width = heads * HEAD
    low = lax.broadcasted_iota(jnp.int32, (COUNT, 128), 1) < HEAD
    zero = jnp.zeros((COUNT, 128), BF16)
    one = jnp.ones((COUNT, 128), BF16)

    def window(index, _):
        rows = pl.ds(pl.multiple_of(index * COUNT, COUNT), COUNT)
        wall = wall_of(index)
        for pair in range(heads // 2):
            lanes = slice(pair * 128, pair * 128 + 128)
            q = qkv[rows, lanes]
            k = qkv[rows, width + pair * 128 : width + pair * 128 + 128]
            v = qkv[rows, 2 * width + pair * 128 : 2 * width + pair * 128 + 128]
            results = []
            for half in range(2):
                mine = low if half == 0 else jnp.logical_not(low)
                scores = lax.dot_general(
                    q, jnp.where(mine, k, zero), (((1,), (1,)), ((), ())), preferred_element_type=F32
                )
                if wall is not None:
                    scores = scores + wall
                powers = jnp.exp(scores - jnp.max(scores, -1, keepdims=True)).astype(BF16)
                results.append(dot(powers, jnp.where(mine, v, one)))
            upper = jnp.where(low, results[0], results[1])
            lower = jnp.where(low, results[1], results[0])
            context[rows, lanes] = (upper / pltpu.roll(lower, HEAD, 1)).astype(BF16)
        return 0

    lax.fori_loop(0, context.shape[0] // COUNT, window, 0)


def late(shape, axis):
    return lax.broadcasted_iota(jnp.int32, shape, axis) >= COUNT // 2


def attend_kernel(lowest, order, grid_ref, *rest):
    if lowest:
        south_ref, east_ref, gain_ref, *buffers, edge_ref, out_ref, weights, x, qkv, context, semaphore = rest
    else:
        gain_ref, *buffers, out_ref, weights, x, qkv, context, semaphore = rest
    tokens, width = x.shape
    share = width // 16
    lat_cut, lon_cut = WIN_LAT // 2, WIN_LON // 2
    columns = grid_ref.shape[2]

    def place(block, index):
        rows = pl.ds(pl.multiple_of(index * share, share), share)
        return [(block, weights.at[rows, :])]

    copies = fetch(order, buffers, place, semaphore)
    across = columns // WIN_LON
    windows = [(0, number) for number in range(across - 1)]
    if lowest:
        windows = [(0, across - 1)] + [(1, number) for number in range(across)]
    for position, (band, number) in enumerate(windows):
        for level in range(WIN_LEV):
            for row in range(WIN_LAT):
                rolled = band * WIN_LAT + row
                target = position * COUNT + (row * WIN_LEV + level) * WIN_LON
                first = number * WIN_LON + lon_cut
                count = min(WIN_LON, columns - first)
                if rolled + lat_cut < grid_ref.shape[1]:
                    piece = grid_ref[level, rolled + lat_cut, first : first + count, :]
                else:
                    piece = south_ref[level, rolled + lat_cut - grid_ref.shape[1], first : first + count, :]
                x[target : target + count, :] = piece.astype(F32)
                if count < WIN_LON:
                    x[target + count : target + WIN_LON, :] = east_ref[level, rolled, :, :].astype(F32)

    normed = normalize(x[...], gain_ref[...]).astype(BF16)
    await_all(copies)
    qkv[:, :width] = (dot(normed, weights[:, :width]) * SCALE).astype(BF16)
    qkv[:, width:] = dot(normed, weights[:, width : 3 * width]).astype(BF16)

    def wall_of(index):
        if not lowest:
            return None
        apart = late((COUNT, COUNT), 0) != late((COUNT, COUNT), 1)
        return jnp.where(apart & (index > 0) & (order[16] > 0), -1e30, 0.0)

    attend_windows(qkv, context, width // HEAD, wall_of)
    done = x[...] + dot(context[...], weights[:, 3 * width :])
    if lowest:
        half = COUNT // 2
        starts = range(COUNT, tokens, COUNT)
        edge = [done[start + half : start + COUNT] for start in starts] + [done[:COUNT], done[tokens - COUNT : tokens - half]]
        edge_ref[...] = jnp.concatenate(edge, 0).astype(BF16)
        out_ref[...] = jnp.concatenate([done[start : start + half] for start in starts[:-1]], 0).astype(BF16)
    else:
        out_ref[...] = done.astype(BF16)


def any_specs(buffers):
    return [pl.BlockSpec(memory_space=pl.ANY)] * len(buffers)


def attend(grid, edges, gain, order, buffers):
    width = grid.shape[-1]
    across = grid.shape[2] // WIN_LON
    tokens = (across + 1 if edges else across - 1) * COUNT
    rest = tokens if not edges else (across - 1) * COUNT // 2
    shapes = [(tokens - rest, width), (rest, width)] if edges else [(rest, width)]
    return pl.pallas_call(
        functools.partial(attend_kernel, bool(edges)),
        out_shape=[jax.ShapeDtypeStruct(shape, BF16) for shape in shapes],
        in_specs=[pl.BlockSpec(memory_space=pltpu.SMEM)]
        + [pl.BlockSpec(memory_space=pltpu.VMEM)] * (2 + len(edges))
        + any_specs(buffers),
        out_specs=[pl.BlockSpec(memory_space=pltpu.VMEM)] * len(shapes),
        scratch_shapes=[
            pltpu.VMEM((width, 4 * width), BF16),
            pltpu.VMEM((tokens, width), F32),
            pltpu.VMEM((tokens, 3 * width), BF16),
            pltpu.VMEM((tokens, width), BF16),
            pltpu.SemaphoreType.DMA,
        ],
        compiler_params=pltpu.CompilerParams(vmem_limit_bytes=VMEM_LIMIT),
        cost_estimate=pl.CostEstimate(
            flops=8 * tokens * width * width + 4 * tokens * COUNT * width,
            bytes_accessed=8 * width * width + 4 * tokens * width,
            transcendentals=tokens * COUNT * (width // HEAD),
        ),
    )(order, grid, *edges, gain.reshape(1, -1), *buffers)


def dense_kernel(parts, edges, order, *rest):
    inputs, (gain_ref, *buffers), outs = rest[:parts], rest[parts : parts + 9], rest[parts + 9 : -3]
    expand, shrink, semaphore = rest[-3:]
    width = gain_ref.shape[1]
    share = width // 16

    def place_expand(block, index):
        rows = pl.ds(pl.multiple_of(index * share, share), share)
        return [(block.at[:, : 4 * width], expand.at[rows, :])]

    def place_shrink(block, index):
        pairs = []
        for part in range(4):
            lanes = slice((4 + part) * width, (5 + part) * width)
            hidden_rows = pl.ds(pl.multiple_of((index * 4 + part) * share, share), share)
            pairs.append((block.at[:, lanes], shrink.at[hidden_rows, :]))
        return pairs

    expand_copies = fetch(order, buffers, place_expand, semaphore.at[0])
    shrink_copies = fetch(order, buffers, place_shrink, semaphore.at[1])
    x = jnp.concatenate([ref[...].astype(F32) for ref in inputs], 0)
    hidden = normalize(x, gain_ref[...]).astype(BF16)
    await_all(expand_copies)
    total = x
    for part in range(4):
        lanes = slice(part * width, (part + 1) * width)
        grown = gelu(dot(hidden, expand[:, lanes])).astype(BF16)
        if part == 0:
            await_all(shrink_copies)
        total = total + dot(grown, shrink[lanes, :])
    start = 0
    for ref in outs[:2] if edges else outs:
        ref[...] = total[start : start + ref.shape[0]].astype(BF16)
        start += ref.shape[0]
    if edges:
        south_ref, _, corner_ref = outs
        last = south_ref.shape[0]
        corner_ref[...] = total[last - corner_ref.shape[0] : last].astype(BF16)


def dense(inputs, gain, order, buffers, edges):
    width = inputs[0].shape[1]
    tokens = sum(item.shape[0] for item in inputs)
    half = COUNT // 2
    shapes = [(tokens - 3 * half, width), (3 * half, width), (half, width)] if edges else [item.shape for item in inputs]
    return pl.pallas_call(
        functools.partial(dense_kernel, len(inputs), edges),
        out_shape=[jax.ShapeDtypeStruct(shape, BF16) for shape in shapes],
        in_specs=[pl.BlockSpec(memory_space=pltpu.SMEM)]
        + [pl.BlockSpec(memory_space=pltpu.VMEM)] * (len(inputs) + 1)
        + any_specs(buffers),
        out_specs=[pl.BlockSpec(memory_space=pltpu.VMEM)] * len(shapes),
        scratch_shapes=[
            pltpu.VMEM((width, 4 * width), BF16),
            pltpu.VMEM((4 * width, width), BF16),
            pltpu.SemaphoreType.DMA((2,)),
        ],
        compiler_params=pltpu.CompilerParams(vmem_limit_bytes=VMEM_LIMIT),
        cost_estimate=pl.CostEstimate(
            flops=16 * tokens * width * width,
            bytes_accessed=16 * width * width + 4 * tokens * width,
            transcendentals=4 * tokens * width,
        ),
    )(order, *inputs, gain.reshape(1, -1), *buffers)


def merge_picks():
    part, row, column, level = np.meshgrid(
        np.arange(4), np.arange(WIN_LAT), np.arange(WIN_LON), np.arange(WIN_LEV), indexing="ij"
    )
    part, level, row, column = (item.reshape(-1) for item in (part, level, row, column))
    fine_row = 2 * row + part % 2 - WIN_LAT // 2
    fine_column = 2 * column + part // 2 - WIN_LON // 2
    number = fine_column // WIN_LON
    column = fine_column % WIN_LON
    half = COUNT // 2
    place = ((fine_row % WIN_LAT) * WIN_LEV + level) * WIN_LON + column
    pick = np.where(fine_row < WIN_LAT, (number + 1) * COUNT, 3 * COUNT + (number + 1) * half) + place
    pick = np.where(fine_row >= 0, pick, -1)
    place = place - half
    south = []
    for coarse in range(3):
        window = 2 * coarse + number
        south.append(np.where((fine_row < 0) & (window >= 0), window * half + place, -1))
    corner = np.where((fine_row < 0) & (number < 0), place, -1)
    shape = (-1, 1)
    return [jnp.asarray(item.astype(np.int32)) for item in (pick.reshape(shape), np.stack(south)[:, :, None], corner.reshape(shape))]


def coarse_kernel(order, quarters, *rest):
    upper_ref, lower_ref, side_ref, south_ref, west_ref, corner_ref = rest[:6]
    pick_ref, south_pick_ref, corner_pick_ref, gain_ref, attend_gain_ref, dense_gain_ref = rest[6:12]
    *buffers, gathered, out_ref = rest[12:-9]
    weights, projections, expand, shrink, qkv, context, mixed, grown, semaphores = rest[-9:]
    width = upper_ref.shape[1]
    share = width // 4
    half = COUNT // 2

    def place(block, index):
        rows = pl.ds(pl.multiple_of(index * share, share), share)
        return [(block, weights.at[rows, :])]

    def rows_of(target):
        return lambda index: target.at[:, pl.ds(pl.multiple_of(index * 16, 16), 16), :]

    def shrink_rows(index):
        return shrink.at[pl.ds(index * 4, 4)]

    copies = fetch(order, buffers, place, semaphores.at[3])
    attend_copies = fetch_quarters(quarters, gathered, 0, rows_of(projections), semaphores.at[0])
    expand_copies = fetch_quarters(quarters, gathered, 4, rows_of(expand), semaphores.at[1])
    shrink_copies = fetch_quarters(quarters, gathered, 8, shrink_rows, semaphores.at[2])

    def chosen(index, source):
        rows = lax.broadcasted_iota(jnp.int32, (index.shape[0], source.shape[0]), 1)
        return dot((rows == index).astype(BF16), source)

    def window(number):
        if number in (-1, 5):
            ref = west_ref if number < 0 else side_ref
            return ref[:COUNT], ref[COUNT:]
        return upper_ref[number * COUNT : number * COUNT + COUNT], lower_ref[number * half : number * half + half]

    results = []
    for coarse in range(3):
        sources = [window(2 * coarse + number) for number in (-1, 0, 1)]
        sources = [item[0] for item in sources] + [item[1] for item in sources]
        quad = chosen(pick_ref[...], jnp.concatenate(sources, 0))
        quad = quad + chosen(south_pick_ref[coarse], south_ref[...])
        if coarse == 0:
            quad = quad + chosen(corner_pick_ref[...], corner_ref[...])
        quarters = [quad[part * COUNT : part * COUNT + COUNT] for part in range(4)]
        mean = sum(jnp.sum(item, -1, keepdims=True) for item in quarters) / (4 * width)
        quarters = [item - mean for item in quarters]
        spread = sum(jnp.sum(item * item, -1, keepdims=True) for item in quarters) / (4 * width)
        level = lax.rsqrt(spread + EPS)
        results.append(
            [
                (item * level * gain_ref[:, part * width : part * width + width]).astype(BF16)
                for part, item in enumerate(quarters)
            ]
        )
    await_all(copies)
    total = None
    for part in range(4):
        normed = jnp.concatenate([item[part] for item in results], 0)
        term = dot(normed, weights[part * width : part * width + width, :])
        total = term if total is None else total + term
    x = total.astype(BF16).astype(F32)
    wide = 2 * width
    normed = normalize(x, attend_gain_ref[...]).astype(BF16)
    await_all(attend_copies)
    qkv[:, :wide] = (dot(normed, projections[0]) * SCALE).astype(BF16)
    qkv[:, wide : 2 * wide] = dot(normed, projections[1]).astype(BF16)
    qkv[:, 2 * wide :] = dot(normed, projections[2]).astype(BF16)
    attend_windows(qkv, context, wide // HEAD, lambda index: None)
    mixed[...] = (x + dot(context[...], projections[3])).astype(BF16)

    hidden = normalize(mixed[...].astype(F32), dense_gain_ref[...]).astype(BF16)
    await_all(expand_copies)
    for part in range(8):
        lanes = slice(part % 2 * width, (part % 2 + 1) * width)
        grown[:, part * width : (part + 1) * width] = gelu(dot(hidden, expand[part // 2, :, lanes])).astype(BF16)
    await_all(shrink_copies)
    pairs = 2 * WIN_LON
    for part in range(2):
        lanes = slice(part * width, (part + 1) * width)
        back = dot(grown[...], shrink[:, :, lanes].reshape(4 * wide, width))
        done = (mixed[:, lanes].astype(F32) + back).astype(BF16)
        for number in range(3):
            for row in range(WIN_LAT):
                start = number * COUNT + row * pairs
                columns = slice(number * WIN_LON, (number + 1) * WIN_LON)
                out_ref[row, columns, :, lanes] = done[start : start + pairs].reshape(WIN_LON, WIN_LEV, width)


def coarse(sources, gains, order, quarters, buffers, gathered):
    width = sources[0].shape[1]
    wide = 2 * width
    tokens = 3 * COUNT
    return pl.pallas_call(
        coarse_kernel,
        out_shape=jax.ShapeDtypeStruct((WIN_LAT, 3 * WIN_LON, WIN_LEV, wide), BF16),
        in_specs=[pl.BlockSpec(memory_space=pltpu.SMEM)] * 2
        + [pl.BlockSpec(memory_space=pltpu.VMEM)] * 12
        + any_specs(buffers)
        + [pl.BlockSpec(memory_space=pl.ANY)],
        out_specs=pl.BlockSpec(memory_space=pltpu.VMEM),
        scratch_shapes=[
            pltpu.VMEM((4 * width, wide), BF16),
            pltpu.VMEM((4, wide, wide), BF16),
            pltpu.VMEM((4, wide, wide), BF16),
            pltpu.VMEM((4 * wide // 16, 16, wide), BF16),
            pltpu.VMEM((tokens, 3 * wide), BF16),
            pltpu.VMEM((tokens, wide), BF16),
            pltpu.VMEM((tokens, wide), BF16),
            pltpu.VMEM((tokens, 4 * wide), BF16),
            pltpu.SemaphoreType.DMA((4,)),
        ],
        compiler_params=pltpu.CompilerParams(vmem_limit_bytes=VMEM_LIMIT),
        cost_estimate=pl.CostEstimate(
            flops=30 * tokens * wide * wide,
            bytes_accessed=28 * wide * wide + 8 * tokens * wide,
            transcendentals=4 * tokens * wide,
        ),
    )(order, quarters, *sources, *merge_picks(), *(gain.reshape(1, -1) for gain in gains), *buffers, gathered)


def pack_kernel(place, heads, back, expand, shrink, wide_heads, wide_back, wide_expand, wide_shrink, *outs):
    first, second, mine, pair = outs
    rows, width = back.shape
    wide = wide_back.shape[1]
    own = pl.ds(pl.multiple_of(place[0] * 16, 16), 16)
    first[:, : 3 * width] = heads[...]
    first[:, 3 * width :] = back[...]
    second[:, : 4 * width] = expand[...]
    for part in range(4):
        second[:, (4 + part) * width : (5 + part) * width] = shrink[part * rows : (part + 1) * rows, :]
    for part in range(3):
        mine[part] = wide_heads[own, part * wide : (part + 1) * wide]
    mine[3] = wide_back[own, :]
    for part in range(4):
        mine[4 + part] = wide_expand[own, part * wide : (part + 1) * wide]
        start = pl.multiple_of(place[0] * 64 + part * 16, 16)
        mine[8 + part] = wide_shrink[pl.ds(start, 16), :]
    pair[0] = mine[...]


def pack(place, *shards):
    rows, width = shards[1].shape
    wide = shards[5].shape[1]
    shapes = [(rows, 4 * width), (rows, 8 * width), (12, 16, wide), (2, 12, 16, wide)]
    return pl.pallas_call(
        pack_kernel,
        out_shape=[jax.ShapeDtypeStruct(shape, BF16) for shape in shapes],
        in_specs=[pl.BlockSpec(memory_space=pltpu.SMEM)] + [pl.BlockSpec(memory_space=pltpu.VMEM)] * len(shards),
        out_specs=[pl.BlockSpec(memory_space=pltpu.VMEM)] * 4,
        compiler_params=pltpu.CompilerParams(vmem_limit_bytes=VMEM_LIMIT),
    )(place, *shards)


LAT = ("x", "zh")
LON = ("y", "zl", "c")


def tie(values, *others):
    return lax.optimization_barrier((values, others))[0]


def step_y(block, steps):
    return lax.ppermute(block, "y", [(place, (place + steps) % 4) for place in range(4)])


def step_z(block, steps):
    return lax.ppermute(block, ("zh", "zl"), [(place, (place + steps) % 4) for place in range(4)])


def step_core(block):
    return lax.ppermute(block, "c", [(0, 1), (1, 0)])


def step_diagonal(block, steps):
    pairs = [(lat * 16 + lon, (lat + steps) % 8 * 16 + (lon + steps) % 16) for lat in range(8) for lon in range(16)]
    return lax.ppermute(block, LAT + LON, pairs)


def spread_order():
    y, zl, c = (lax.axis_index(name) for name in LON)
    places = []
    for other_core in range(2):
        for other_z in range(2):
            for steps in (0, 2, 3, 1):
                places.append(((y + steps) % 4) * 4 + (zl ^ other_z) * 2 + (c ^ other_core))
    return jnp.stack(places).astype(jnp.int32)


def quarter_order():
    zl = lax.axis_index("zl")
    x, y, c, other = jnp.meshgrid(jnp.arange(4), jnp.arange(4), jnp.arange(2), jnp.arange(2), indexing="ij")
    block = y * 4 + (zl ^ other) * 2 + c
    return (block * 4 + x).reshape(-1).astype(jnp.int32)


def spread_y(shard):
    return [shard[None], step_y(shard, 2)[None], step_y(shard, 1)[None], step_y(shard, -1)[None]]


def paired(near):
    return [jnp.concatenate(near[:2]), jnp.concatenate(near[2:])]


def spread_z(pairs):
    return [step_z(pairs[0], 1), step_z(pairs[1], -1)]


def spread_core(pairs):
    return [step_core(block) for block in pairs]


def fence(*values):
    return lax.optimization_barrier(values)


def passed_along(value, axes, steps):
    count = 1
    for axis in axes:
        count *= lax.axis_size(axis)
    pairs = [(source, (source + steps) % count) for source in range(count)]
    return lax.ppermute(value, axes, pairs)


def per_device(
    latents,
    attend_gain,
    packed_heads,
    heads_back,
    dense_gain,
    expand_weight,
    shrink_weight,
    merge_gain,
    merge_weight,
    coarse_gain,
    coarse_heads,
    coarse_back,
    coarse_scale,
    coarse_expand,
    coarse_shrink,
):
    lat_cut, lon_cut = WIN_LAT // 2, WIN_LON // 2
    order = quarter_order()
    place = lax.axis_index("x") * 2 + lax.axis_index("zh")
    last = (place == lax.axis_size("x") * 2 - 1).astype(jnp.int32)
    places = jnp.concatenate([spread_order(), last[None]])

    first, second, mine, pair = pack(
        lax.axis_index("x")[None].astype(jnp.int32),
        packed_heads,
        heads_back,
        expand_weight,
        shrink_weight,
        coarse_heads,
        coarse_back,
        coarse_expand,
        coarse_shrink,
    )
    other = step_z(mine, 1)
    near = spread_y(first)
    near, pair, other = fence(near, pair, other)
    gathered = lax.all_gather(pair.at[1].set(other), ("x", "y", "c"), axis=0, tiled=False)
    a_near = paired(near)
    a_far = spread_z(a_near)
    a_mate = spread_core(a_near)
    east_edge = passed_along(tie(latents[:, lat_cut:, :lon_cut], a_near), LON, -1)
    a_near, a_far, a_mate, east_edge = fence(a_near, a_far, a_mate, east_edge)
    a_mate += spread_core(a_far)
    south_edge = passed_along(tie(latents[:, :lat_cut], a_near), LAT, -1)
    corner = step_diagonal(tie(latents[:, :lat_cut, :lon_cut], a_near), -1)
    near = spread_y(tie(second, a_mate))
    fine_attend = a_near + a_far + a_mate

    (upper,) = attend(latents, [], attend_gain, places, fine_attend)
    near, upper, south_edge, corner = fence(near, upper, south_edge, corner)
    east_edge = jnp.concatenate([east_edge, corner], 1)
    b_near = paired(near)
    b_far = spread_z(b_near)
    near = spread_y(tie(merge_weight, upper))
    edge, lower = attend(tie(latents, upper), [south_edge, east_edge], attend_gain, places, fine_attend)
    near, b_near, b_far, edge, lower = fence(near, b_near, b_far, edge, lower)
    b_mate = spread_core(b_near) + spread_core(b_far)
    b_mate, near = fence(b_mate, near)
    c_near = paired(near)
    c_far = spread_z(c_near)
    c_mate = spread_core(c_near)

    fine_dense = b_near + b_far + b_mate
    south, side, corner = dense([tie(edge, c_near)], dense_gain, places, fine_dense, True)
    c_near, c_mate, south, side, corner = fence(c_near, c_mate, south, side, corner)
    south = passed_along(south, LAT, 1)
    west = passed_along(side, LON, 1)
    corner = step_diagonal(corner, 1)
    upper, lower = dense(tie([upper, lower], side), dense_gain, places, fine_dense, False)
    upper, lower, c_far, south, west, corner = fence(upper, lower, c_far, south, west, corner)
    merging = c_near + c_far + c_mate + spread_core(c_far)
    sources = [upper, lower, side, south, west, corner]
    gains = [merge_gain, coarse_gain, coarse_scale]
    finished = coarse(sources, gains, places, order, merging, gathered)
    return finished.transpose(2, 0, 1, 3)


def solution(mesh):
    fine_mesh = Mesh(mesh.devices.reshape(4, 2, 4, 2, 2), ("x", "zh", "y", "zl", "c"))
    rows = P(LON, None)
    grid = P(None, LAT, LON, None)
    in_specs = (grid, P(), rows, rows, P(), rows, rows, P(), rows, P(), rows, rows, P(), rows, rows)
    return jax.shard_map(
        per_device, mesh=fine_mesh, in_specs=in_specs, out_specs=grid, check_vma=False
    )
```

```python
import functools
import jax
import jax.numpy as jnp
import numpy as np
from jax import lax
from jax.experimental import pallas as pl
from jax.experimental.pallas import tpu as pltpu
from jax.sharding import Mesh, PartitionSpec as P

HEAD = 64
COUNT = 144
WIN_LEV = 2
WIN_LAT = 6
WIN_LON = 12
EPS = 1e-05
SCALE = 0.125
VMEM_LIMIT = 56 * 1024 * 1024
F32 = jnp.float32
BF16 = jnp.bfloat16


def normalize(values, gain):
    center = values - jnp.mean(values, -1, keepdims=True)
    spread = jnp.mean(center * center, -1, keepdims=True)
    return center * lax.rsqrt(spread + EPS) * gain


def dot(left, right):
    return jnp.dot(left, right, preferred_element_type=F32)


def gelu(x):
    return 0.5 * x * (1.0 + lax.erf(x * (0.5 ** 0.5)))


def fetch(order, buffers, place, semaphore):
    copies = []
    position = 0
    for buffer in buffers:
        for item in range(buffer.shape[0]):
            for source, target in place(buffer.at[item], order[position]):
                copies.append(pltpu.make_async_copy(source, target, semaphore))
            position += 1
    for copy in copies:
        copy.start()
    return copies


def await_all(copies):
    for copy in copies:
        copy.wait()


def fetch_quarters(order, gathered, first, place, semaphore):
    copies = []
    for position in range(gathered.shape[0]):
        for other in range(2):
            source = gathered.at[position, other, pl.ds(first, 4)]
            copies.append(pltpu.make_async_copy(source, place(order[2 * position + other]), semaphore))
    for copy in copies:
        copy.start()
    return copies


def attend_windows(qkv, context, heads, wall_of):
    width = heads * HEAD
    low = lax.broadcasted_iota(jnp.int32, (COUNT, 128), 1) < HEAD
    zero = jnp.zeros((COUNT, 128), BF16)
    one = jnp.ones((COUNT, 128), BF16)

    def window(index, _):
        rows = pl.ds(pl.multiple_of(index * COUNT, COUNT), COUNT)
        wall = wall_of(index)
        for pair in range(heads // 2):
            lanes = slice(pair * 128, pair * 128 + 128)
            q = qkv[rows, lanes]
            k = qkv[rows, width + pair * 128 : width + pair * 128 + 128]
            v = qkv[rows, 2 * width + pair * 128 : 2 * width + pair * 128 + 128]
            results = []
            for half in range(2):
                mine = low if half == 0 else jnp.logical_not(low)
                scores = lax.dot_general(
                    q, jnp.where(mine, k, zero), (((1,), (1,)), ((), ())), preferred_element_type=F32
                )
                if wall is not None:
                    scores = scores + wall
                powers = jnp.exp(scores - jnp.max(scores, -1, keepdims=True)).astype(BF16)
                results.append(dot(powers, jnp.where(mine, v, one)))
            upper = jnp.where(low, results[0], results[1])
            lower = jnp.where(low, results[1], results[0])
            context[rows, lanes] = (upper / pltpu.roll(lower, HEAD, 1)).astype(BF16)
        return 0

    lax.fori_loop(0, context.shape[0] // COUNT, window, 0)


def late(shape, axis):
    return lax.broadcasted_iota(jnp.int32, shape, axis) >= COUNT // 2


def attend_kernel(lowest, order, grid_ref, *rest):
    if lowest:
        south_ref, east_ref, gain_ref, *buffers, edge_ref, out_ref, weights, x, qkv, context, semaphore = rest
    else:
        gain_ref, *buffers, out_ref, weights, x, qkv, context, semaphore = rest
    tokens, width = x.shape
    share = width // 16
    lat_cut, lon_cut = WIN_LAT // 2, WIN_LON // 2
    columns = grid_ref.shape[2]

    def place(block, index):
        rows = pl.ds(pl.multiple_of(index * share, share), share)
        return [(block, weights.at[rows, :])]

    copies = fetch(order, buffers, place, semaphore)
    across = columns // WIN_LON
    windows = [(0, number) for number in range(across - 1)]
    if lowest:
        windows = [(0, across - 1)] + [(1, number) for number in range(across)]
    for position, (band, number) in enumerate(windows):
        for level in range(WIN_LEV):
            for row in range(WIN_LAT):
                rolled = band * WIN_LAT + row
                target = position * COUNT + (row * WIN_LEV + level) * WIN_LON
                first = number * WIN_LON + lon_cut
                count = min(WIN_LON, columns - first)
                if rolled + lat_cut < grid_ref.shape[1]:
                    piece = grid_ref[level, rolled + lat_cut, first : first + count, :]
                else:
                    piece = south_ref[level, rolled + lat_cut - grid_ref.shape[1], first : first + count, :]
                x[target : target + count, :] = piece.astype(F32)
                if count < WIN_LON:
                    x[target + count : target + WIN_LON, :] = east_ref[level, rolled, :, :].astype(F32)

    normed = normalize(x[...], gain_ref[...]).astype(BF16)
    await_all(copies)
    qkv[:, :width] = (dot(normed, weights[:, :width]) * SCALE).astype(BF16)
    qkv[:, width:] = dot(normed, weights[:, width : 3 * width]).astype(BF16)

    def wall_of(index):
        if not lowest:
            return None
        apart = late((COUNT, COUNT), 0) != late((COUNT, COUNT), 1)
        return jnp.where(apart & (index > 0) & (order[16] > 0), -1e30, 0.0)

    attend_windows(qkv, context, width // HEAD, wall_of)
    done = x[...] + dot(context[...], weights[:, 3 * width :])
    if lowest:
        half = COUNT // 2
        starts = range(COUNT, tokens, COUNT)
        edge = [done[start + half : start + COUNT] for start in starts] + [done[:COUNT], done[tokens - COUNT : tokens - half]]
        edge_ref[...] = jnp.concatenate(edge, 0).astype(BF16)
        out_ref[...] = jnp.concatenate([done[start : start + half] for start in starts[:-1]], 0).astype(BF16)
    else:
        out_ref[...] = done.astype(BF16)


def any_specs(buffers):
    return [pl.BlockSpec(memory_space=pl.ANY)] * len(buffers)


def attend(grid, edges, gain, order, buffers):
    width = grid.shape[-1]
    across = grid.shape[2] // WIN_LON
    tokens = (across + 1 if edges else across - 1) * COUNT
    rest = tokens if not edges else (across - 1) * COUNT // 2
    shapes = [(tokens - rest, width), (rest, width)] if edges else [(rest, width)]
    return pl.pallas_call(
        functools.partial(attend_kernel, bool(edges)),
        out_shape=[jax.ShapeDtypeStruct(shape, BF16) for shape in shapes],
        in_specs=[pl.BlockSpec(memory_space=pltpu.SMEM)]
        + [pl.BlockSpec(memory_space=pltpu.VMEM)] * (2 + len(edges))
        + any_specs(buffers),
        out_specs=[pl.BlockSpec(memory_space=pltpu.VMEM)] * len(shapes),
        scratch_shapes=[
            pltpu.VMEM((width, 4 * width), BF16),
            pltpu.VMEM((tokens, width), F32),
            pltpu.VMEM((tokens, 3 * width), BF16),
            pltpu.VMEM((tokens, width), BF16),
            pltpu.SemaphoreType.DMA,
        ],
        compiler_params=pltpu.CompilerParams(vmem_limit_bytes=VMEM_LIMIT),
        cost_estimate=pl.CostEstimate(
            flops=8 * tokens * width * width + 4 * tokens * COUNT * width,
            bytes_accessed=8 * width * width + 4 * tokens * width,
            transcendentals=tokens * COUNT * (width // HEAD),
        ),
    )(order, grid, *edges, gain.reshape(1, -1), *buffers)


def dense_kernel(parts, edges, order, *rest):
    inputs, (gain_ref, *buffers), outs = rest[:parts], rest[parts : parts + 9], rest[parts + 9 : -3]
    expand, shrink, semaphore = rest[-3:]
    width = gain_ref.shape[1]
    share = width // 16

    def place_expand(block, index):
        rows = pl.ds(pl.multiple_of(index * share, share), share)
        return [(block.at[:, : 4 * width], expand.at[rows, :])]

    def place_shrink(block, index):
        pairs = []
        for part in range(4):
            lanes = slice((4 + part) * width, (5 + part) * width)
            hidden_rows = pl.ds(pl.multiple_of((index * 4 + part) * share, share), share)
            pairs.append((block.at[:, lanes], shrink.at[hidden_rows, :]))
        return pairs

    expand_copies = fetch(order, buffers, place_expand, semaphore.at[0])
    shrink_copies = fetch(order, buffers, place_shrink, semaphore.at[1])
    x = jnp.concatenate([ref[...].astype(F32) for ref in inputs], 0)
    hidden = normalize(x, gain_ref[...]).astype(BF16)
    await_all(expand_copies)
    total = x
    for part in range(4):
        lanes = slice(part * width, (part + 1) * width)
        grown = gelu(dot(hidden, expand[:, lanes])).astype(BF16)
        if part == 0:
            await_all(shrink_copies)
        total = total + dot(grown, shrink[lanes, :])
    start = 0
    for ref in outs[:2] if edges else outs:
        ref[...] = total[start : start + ref.shape[0]].astype(BF16)
        start += ref.shape[0]
    if edges:
        south_ref, _, corner_ref = outs
        last = south_ref.shape[0]
        corner_ref[...] = total[last - corner_ref.shape[0] : last].astype(BF16)


def dense(inputs, gain, order, buffers, edges):
    width = inputs[0].shape[1]
    tokens = sum(item.shape[0] for item in inputs)
    half = COUNT // 2
    shapes = [(tokens - 3 * half, width), (3 * half, width), (half, width)] if edges else [item.shape for item in inputs]
    return pl.pallas_call(
        functools.partial(dense_kernel, len(inputs), edges),
        out_shape=[jax.ShapeDtypeStruct(shape, BF16) for shape in shapes],
        in_specs=[pl.BlockSpec(memory_space=pltpu.SMEM)]
        + [pl.BlockSpec(memory_space=pltpu.VMEM)] * (len(inputs) + 1)
        + any_specs(buffers),
        out_specs=[pl.BlockSpec(memory_space=pltpu.VMEM)] * len(shapes),
        scratch_shapes=[
            pltpu.VMEM((width, 4 * width), BF16),
            pltpu.VMEM((4 * width, width), BF16),
            pltpu.SemaphoreType.DMA((2,)),
        ],
        compiler_params=pltpu.CompilerParams(vmem_limit_bytes=VMEM_LIMIT),
        cost_estimate=pl.CostEstimate(
            flops=16 * tokens * width * width,
            bytes_accessed=16 * width * width + 4 * tokens * width,
            transcendentals=4 * tokens * width,
        ),
    )(order, *inputs, gain.reshape(1, -1), *buffers)


def merge_picks():
    part, row, column, level = np.meshgrid(
        np.arange(4), np.arange(WIN_LAT), np.arange(WIN_LON), np.arange(WIN_LEV), indexing="ij"
    )
    part, level, row, column = (item.reshape(-1) for item in (part, level, row, column))
    fine_row = 2 * row + part % 2 - WIN_LAT // 2
    fine_column = 2 * column + part // 2 - WIN_LON // 2
    number = fine_column // WIN_LON
    column = fine_column % WIN_LON
    half = COUNT // 2
    place = ((fine_row % WIN_LAT) * WIN_LEV + level) * WIN_LON + column
    pick = np.where(fine_row < WIN_LAT, (number + 1) * COUNT, 3 * COUNT + (number + 1) * half) + place
    pick = np.where(fine_row >= 0, pick, -1)
    place = place - half
    south = []
    for coarse in range(3):
        window = 2 * coarse + number
        south.append(np.where((fine_row < 0) & (window >= 0), window * half + place, -1))
    corner = np.where((fine_row < 0) & (number < 0), place, -1)
    shape = (-1, 1)
    return [jnp.asarray(item.astype(np.int32)) for item in (pick.reshape(shape), np.stack(south)[:, :, None], corner.reshape(shape))]


def coarse_kernel(order, quarters, *rest):
    upper_ref, lower_ref, side_ref, south_ref, west_ref, corner_ref = rest[:6]
    pick_ref, south_pick_ref, corner_pick_ref, gain_ref, attend_gain_ref, dense_gain_ref = rest[6:12]
    *buffers, gathered, out_ref = rest[12:-9]
    weights, projections, expand, shrink, qkv, context, mixed, grown, semaphores = rest[-9:]
    width = upper_ref.shape[1]
    share = width // 4
    half = COUNT // 2

    def place(block, index):
        rows = pl.ds(pl.multiple_of(index * share, share), share)
        return [(block, weights.at[rows, :])]

    def rows_of(target):
        return lambda index: target.at[:, pl.ds(pl.multiple_of(index * 16, 16), 16), :]

    def shrink_rows(index):
        return shrink.at[pl.ds(index * 4, 4)]

    copies = fetch(order, buffers, place, semaphores.at[3])
    attend_copies = fetch_quarters(quarters, gathered, 0, rows_of(projections), semaphores.at[0])
    expand_copies = fetch_quarters(quarters, gathered, 4, rows_of(expand), semaphores.at[1])
    shrink_copies = fetch_quarters(quarters, gathered, 8, shrink_rows, semaphores.at[2])

    def chosen(index, source):
        rows = lax.broadcasted_iota(jnp.int32, (index.shape[0], source.shape[0]), 1)
        return dot((rows == index).astype(BF16), source)

    def window(number):
        if number in (-1, 5):
            ref = west_ref if number < 0 else side_ref
            return ref[:COUNT], ref[COUNT:]
        return upper_ref[number * COUNT : number * COUNT + COUNT], lower_ref[number * half : number * half + half]

    results = []
    for coarse in range(3):
        sources = [window(2 * coarse + number) for number in (-1, 0, 1)]
        sources = [item[0] for item in sources] + [item[1] for item in sources]
        quad = chosen(pick_ref[...], jnp.concatenate(sources, 0))
        quad = quad + chosen(south_pick_ref[coarse], south_ref[...])
        if coarse == 0:
            quad = quad + chosen(corner_pick_ref[...], corner_ref[...])
        quarters = [quad[part * COUNT : part * COUNT + COUNT] for part in range(4)]
        mean = sum(jnp.sum(item, -1, keepdims=True) for item in quarters) / (4 * width)
        quarters = [item - mean for item in quarters]
        spread = sum(jnp.sum(item * item, -1, keepdims=True) for item in quarters) / (4 * width)
        level = lax.rsqrt(spread + EPS)
        results.append(
            [
                (item * level * gain_ref[:, part * width : part * width + width]).astype(BF16)
                for part, item in enumerate(quarters)
            ]
        )
    await_all(copies)
    total = None
    for part in range(4):
        normed = jnp.concatenate([item[part] for item in results], 0)
        term = dot(normed, weights[part * width : part * width + width, :])
        total = term if total is None else total + term
    x = total.astype(BF16).astype(F32)
    wide = 2 * width
    normed = normalize(x, attend_gain_ref[...]).astype(BF16)
    await_all(attend_copies)
    qkv[:, :wide] = (dot(normed, projections[0]) * SCALE).astype(BF16)
    qkv[:, wide : 2 * wide] = dot(normed, projections[1]).astype(BF16)
    qkv[:, 2 * wide :] = dot(normed, projections[2]).astype(BF16)
    attend_windows(qkv, context, wide // HEAD, lambda index: None)
    mixed[...] = (x + dot(context[...], projections[3])).astype(BF16)

    hidden = normalize(mixed[...].astype(F32), dense_gain_ref[...]).astype(BF16)
    await_all(expand_copies)
    for part in range(8):
        lanes = slice(part % 2 * width, (part % 2 + 1) * width)
        grown[:, part * width : (part + 1) * width] = gelu(dot(hidden, expand[part // 2, :, lanes])).astype(BF16)
    await_all(shrink_copies)
    pairs = 2 * WIN_LON
    for part in range(2):
        lanes = slice(part * width, (part + 1) * width)
        back = dot(grown[...], shrink[:, :, lanes].reshape(4 * wide, width))
        done = (mixed[:, lanes].astype(F32) + back).astype(BF16)
        for number in range(3):
            for row in range(WIN_LAT):
                start = number * COUNT + row * pairs
                columns = slice(number * WIN_LON, (number + 1) * WIN_LON)
                out_ref[row, columns, :, lanes] = done[start : start + pairs].reshape(WIN_LON, WIN_LEV, width)


def coarse(sources, gains, order, quarters, buffers, gathered):
    width = sources[0].shape[1]
    wide = 2 * width
    tokens = 3 * COUNT
    return pl.pallas_call(
        coarse_kernel,
        out_shape=jax.ShapeDtypeStruct((WIN_LAT, 3 * WIN_LON, WIN_LEV, wide), BF16),
        in_specs=[pl.BlockSpec(memory_space=pltpu.SMEM)] * 2
        + [pl.BlockSpec(memory_space=pltpu.VMEM)] * 12
        + any_specs(buffers)
        + [pl.BlockSpec(memory_space=pl.ANY)],
        out_specs=pl.BlockSpec(memory_space=pltpu.VMEM),
        scratch_shapes=[
            pltpu.VMEM((4 * width, wide), BF16),
            pltpu.VMEM((4, wide, wide), BF16),
            pltpu.VMEM((4, wide, wide), BF16),
            pltpu.VMEM((4 * wide // 16, 16, wide), BF16),
            pltpu.VMEM((tokens, 3 * wide), BF16),
            pltpu.VMEM((tokens, wide), BF16),
            pltpu.VMEM((tokens, wide), BF16),
            pltpu.VMEM((tokens, 4 * wide), BF16),
            pltpu.SemaphoreType.DMA((4,)),
        ],
        compiler_params=pltpu.CompilerParams(vmem_limit_bytes=VMEM_LIMIT),
        cost_estimate=pl.CostEstimate(
            flops=30 * tokens * wide * wide,
            bytes_accessed=28 * wide * wide + 8 * tokens * wide,
            transcendentals=4 * tokens * wide,
        ),
    )(order, quarters, *sources, *merge_picks(), *(gain.reshape(1, -1) for gain in gains), *buffers, gathered)


def pack_kernel(place, heads, back, expand, shrink, wide_heads, wide_back, wide_expand, wide_shrink, *outs):
    first, second, mine, pair = outs
    rows, width = back.shape
    wide = wide_back.shape[1]
    own = pl.ds(pl.multiple_of(place[0] * 16, 16), 16)
    first[:, : 3 * width] = heads[...]
    first[:, 3 * width :] = back[...]
    second[:, : 4 * width] = expand[...]
    for part in range(4):
        second[:, (4 + part) * width : (5 + part) * width] = shrink[part * rows : (part + 1) * rows, :]
    for part in range(3):
        mine[part] = wide_heads[own, part * wide : (part + 1) * wide]
    mine[3] = wide_back[own, :]
    for part in range(4):
        mine[4 + part] = wide_expand[own, part * wide : (part + 1) * wide]
        start = pl.multiple_of(place[0] * 64 + part * 16, 16)
        mine[8 + part] = wide_shrink[pl.ds(start, 16), :]
    pair[0] = mine[...]


def pack(place, *shards):
    rows, width = shards[1].shape
    wide = shards[5].shape[1]
    shapes = [(rows, 4 * width), (rows, 8 * width), (12, 16, wide), (2, 12, 16, wide)]
    return pl.pallas_call(
        pack_kernel,
        out_shape=[jax.ShapeDtypeStruct(shape, BF16) for shape in shapes],
        in_specs=[pl.BlockSpec(memory_space=pltpu.SMEM)] + [pl.BlockSpec(memory_space=pltpu.VMEM)] * len(shards),
        out_specs=[pl.BlockSpec(memory_space=pltpu.VMEM)] * 4,
        compiler_params=pltpu.CompilerParams(vmem_limit_bytes=VMEM_LIMIT),
    )(place, *shards)


LAT = ("x", "zh")
LON = ("y", "zl", "c")


def tie(values, *others):
    return lax.optimization_barrier((values, others))[0]


def step_y(block, steps):
    return lax.ppermute(block, "y", [(place, (place + steps) % 4) for place in range(4)])


def step_z(block, steps):
    return lax.ppermute(block, ("zh", "zl"), [(place, (place + steps) % 4) for place in range(4)])


def step_core(block):
    return lax.ppermute(block, "c", [(0, 1), (1, 0)])


def step_diagonal(block, steps):
    pairs = [(lat * 16 + lon, (lat + steps) % 8 * 16 + (lon + steps) % 16) for lat in range(8) for lon in range(16)]
    return lax.ppermute(block, LAT + LON, pairs)


def spread_order():
    y, zl, c = (lax.axis_index(name) for name in LON)
    places = []
    for other_core in range(2):
        for other_z in range(2):
            for steps in (0, 2, 3, 1):
                places.append(((y + steps) % 4) * 4 + (zl ^ other_z) * 2 + (c ^ other_core))
    return jnp.stack(places).astype(jnp.int32)


def quarter_order():
    zl = lax.axis_index("zl")
    x, y, c, other = jnp.meshgrid(jnp.arange(4), jnp.arange(4), jnp.arange(2), jnp.arange(2), indexing="ij")
    block = y * 4 + (zl ^ other) * 2 + c
    return (block * 4 + x).reshape(-1).astype(jnp.int32)


def spread_y(shard):
    return [shard[None], step_y(shard, 2)[None], step_y(shard, 1)[None], step_y(shard, -1)[None]]


def paired(near):
    return [jnp.concatenate(near[:2]), jnp.concatenate(near[2:])]


def spread_z(pairs):
    return [step_z(pairs[0], 1), step_z(pairs[1], -1)]


def spread_core(pairs):
    return [step_core(block) for block in pairs]


def fence(*values):
    return lax.optimization_barrier(values)


def passed_along(value, axes, steps):
    count = 1
    for axis in axes:
        count *= lax.axis_size(axis)
    pairs = [(source, (source + steps) % count) for source in range(count)]
    return lax.ppermute(value, axes, pairs)


def per_device(
    latents,
    attend_gain,
    packed_heads,
    heads_back,
    dense_gain,
    expand_weight,
    shrink_weight,
    merge_gain,
    merge_weight,
    coarse_gain,
    coarse_heads,
    coarse_back,
    coarse_scale,
    coarse_expand,
    coarse_shrink,
):
    lat_cut, lon_cut = WIN_LAT // 2, WIN_LON // 2
    order = quarter_order()
    place = lax.axis_index("x") * 2 + lax.axis_index("zh")
    last = (place == lax.axis_size("x") * 2 - 1).astype(jnp.int32)
    places = jnp.concatenate([spread_order(), last[None]])

    first, second, mine, pair = pack(
        lax.axis_index("x")[None].astype(jnp.int32),
        packed_heads,
        heads_back,
        expand_weight,
        shrink_weight,
        coarse_heads,
        coarse_back,
        coarse_expand,
        coarse_shrink,
    )
    other = step_z(mine, 1)
    edges = [latents[:, lat_cut:, :lon_cut], latents[:, :lat_cut], latents[:, :lat_cut, :lon_cut]]
    first, edges, order, places = fence(first, edges, order, places)
    near = spread_y(first)
    near, pair, other = fence(near, pair, other)
    gathered = lax.all_gather(pair.at[1].set(other), ("x", "y", "c"), axis=0, tiled=False)
    a_near = paired(near)
    a_far = spread_z(a_near)
    a_mate = spread_core(a_near)
    east_edge = passed_along(tie(edges[0], a_near), LON, -1)
    a_near, a_far, a_mate, east_edge = fence(a_near, a_far, a_mate, east_edge)
    a_mate += spread_core(a_far)
    south_edge = passed_along(tie(edges[1], a_near), LAT, -1)
    corner = step_diagonal(tie(edges[2], a_near), -1)
    near = spread_y(tie(second, a_mate))
    fine_attend = a_near + a_far + a_mate

    (upper,) = attend(latents, [], attend_gain, places, fine_attend)
    near, upper, south_edge, corner = fence(near, upper, south_edge, corner)
    east_edge = jnp.concatenate([east_edge, corner], 1)
    b_near = paired(near)
    b_far = spread_z(b_near)
    near = spread_y(tie(merge_weight, upper))
    edge, lower = attend(tie(latents, upper), [south_edge, east_edge], attend_gain, places, fine_attend)
    near, b_near, b_far, edge, lower = fence(near, b_near, b_far, edge, lower)
    b_mate = spread_core(b_near) + spread_core(b_far)
    b_mate, near = fence(b_mate, near)
    c_near = paired(near)
    c_far = spread_z(c_near)
    c_mate = spread_core(c_near)

    fine_dense = b_near + b_far + b_mate
    south, side, corner = dense([tie(edge, c_near)], dense_gain, places, fine_dense, True)
    c_near, c_mate, south, side, corner = fence(c_near, c_mate, south, side, corner)
    south = passed_along(south, LAT, 1)
    west = passed_along(side, LON, 1)
    corner = step_diagonal(corner, 1)
    upper, lower = dense(tie([upper, lower], side), dense_gain, places, fine_dense, False)
    upper, lower, c_far, south, west, corner = fence(upper, lower, c_far, south, west, corner)
    merging = c_near + c_far + c_mate + spread_core(c_far)
    sources = [upper, lower, side, south, west, corner]
    gains = [merge_gain, coarse_gain, coarse_scale]
    finished = coarse(sources, gains, places, order, merging, gathered)
    return finished.transpose(2, 0, 1, 3)


def solution(mesh):
    fine_mesh = Mesh(mesh.devices.reshape(4, 2, 4, 2, 2), ("x", "zh", "y", "zl", "c"))
    rows = P(LON, None)
    grid = P(None, LAT, LON, None)
    in_specs = (grid, P(), rows, rows, P(), rows, rows, P(), rows, P(), rows, rows, P(), rows, rows)
    return jax.shard_map(
        per_device, mesh=fine_mesh, in_specs=in_specs, out_specs=grid, check_vma=False
    )
```
